256 devices in a mesh: seq: 32 (over y, z_hi, core), head: 8 (over x, z_lo).
Axes of the slice: x: 4, y: 4, z: 8 (z_hi: 4, z_lo: 2; z = z_hi * 2 + z_lo), core: 2. Of those that a mesh axis runs over, the one named last changes fastest.
Arguments:
- prompt_qkv: bfloat16 [3, 2048, 4096], P(None, 'seq', 'head'), may hold values from -16 to 16
- prompt_grad: bfloat16 [2048, 4096], P('seq', 'head'), may hold values from -6 to 6
- comp_qkv: bfloat16 [3, 32, 256, 4096], P(None, 'seq', 'head'), may hold values from -16 to 16
- comp_grad: bfloat16 [32, 256, 4096], P('seq', 'head'), may hold values from -6 to 6
- lengths: int32 [32], P('seq'), may hold values from 64 to 256, as said below
- keep_mask: int32 [32, 256], P('seq'), may hold values 0 or 1
Outputs:
- prompt_out: bfloat16 [2048, 4096], P('seq', 'head')
- comp_out: bfloat16 [32, 256, 4096], P('seq', 'head')
- prompt_dqkv: bfloat16 [3, 2048, 4096], P(None, 'seq', 'head')
- comp_dqkv: bfloat16 [3, 32, 256, 4096], P(None, 'seq', 'head')
The draws below stay inside these ranges and needn't reach their ends.
Inputs may be any that keep to these rules, and one draw needn't show every extreme that they name: `lengths`: every length lies in 64..256, and at least one completion has length 256.
All inputs are finite; a program needn't handle non-finite values. No bound on the sum of `keep_mask` on one device may be relied on, other than what follows from the above.
Results may differ from the reference program's by a relative error of at most 0.033.
Values may be sent and summed in bfloat16 or wider, within the bound.
A program may use at most 128 MiB of HBM per device.

```python
import math
import jax
import jax.numpy as jnp
from jax import lax

HEADS = 32
HEAD_DIM = 128
D = 4096
L = 256
PROMPT = 2048
COMPS = 32


def draw_prompt_qkv(key, part):
    key = jax.random.fold_in(key, 1)
    first = jax.random.fold_in(key, 0)
    base = jax.random.truncated_normal(first, -5.0, 5.0, (3, PROMPT, D), jnp.float32)
    return base.astype(jnp.bfloat16)


def draw_comp_qkv(key, part):
    key = jax.random.fold_in(key, 2)
    first = jax.random.fold_in(key, 0)
    base = jax.random.truncated_normal(first, -5.0, 5.0, (3, COMPS, L, D), jnp.float32)
    return base.astype(jnp.bfloat16)


def draw_lengths(key, part):
    key = jax.random.fold_in(key, 7)
    first, second = jax.random.split(key)
    drawn = jax.random.randint(first, (COMPS,), L // 4, L + 1)
    pick = jax.random.randint(second, (), 0, COMPS)
    return drawn.at[pick].set(L).astype(jnp.int32)


def plant(values, key, low, high):
    shape = values.shape
    place = [jax.random.randint(jax.random.fold_in(key, axis), (), 0, shape[axis]) for axis in range(len(shape))]
    values = values.at[tuple(place)].set(low)
    longest = shape.index(max(shape))
    place[longest] = (place[longest] + 1) % shape[longest]
    return values.at[tuple(place)].set(high)


def block_levels(rng, shape, cuts, least, largest):
    level, own = 1.0, jax.random.fold_in(rng, 6)
    for axis_at, blocks in cuts:
        heights = jnp.exp(jax.random.uniform(jax.random.fold_in(own, axis_at), (blocks,), jnp.float32, least / len(cuts), largest / len(cuts)))
        level = level * jnp.repeat(heights, shape[axis_at] // blocks).reshape([-1 if axis == axis_at else 1 for axis in range(len(shape))])
    return level


def noise(stream_key, shape, width, reach, cuts=(), held_as=jnp.bfloat16):
    gain = block_levels(stream_key, shape, cuts, -0.22, 0.18) if cuts else 1.0
    values = jax.random.normal(stream_key, shape, jnp.float32) * width * gain
    return jnp.minimum(jnp.maximum(values, -reach), reach).astype(held_as)


def setup_inputs(seed: int = 0) -> dict:
    key_list = jax.random.split(jax.random.key(seed), 7)
    return {
        "prompt_qkv": draw_prompt_qkv(jax.random.fold_in(key_list[6], 71), 0),
        "prompt_grad": noise(key_list[1], (PROMPT, D), 1.0, 6.0, ((0, 32), (1, 8))),
        "comp_qkv": draw_comp_qkv(jax.random.fold_in(key_list[6], 71), 0),
        "comp_grad": noise(key_list[3], (COMPS, L, D), 1.0, 6.0, ((0, 32), (1, 8))),
        "lengths": draw_lengths(jax.random.fold_in(key_list[6], 71), 0),
        "keep_mask": plant((jax.random.randint(key_list[5], (COMPS, L), 0, 4) < 3).astype(jnp.int32), jax.random.fold_in(key_list[5], 1), 0, 1),
    }


def reference(prompt_qkv, prompt_grad, comp_qkv, comp_grad, lengths, keep_mask):
    factor = 1.0 / math.sqrt(HEAD_DIM)
    prompt_len = prompt_grad.shape[0]

    def by_head(x):
        return jnp.transpose(x.reshape(prompt_len, HEADS, HEAD_DIM), (1, 0, 2))

    def self_head(items):
        query, keys, values, cot = items
        score = jnp.dot(query, keys.T, preferred_element_type=jnp.float32) * factor
        top = lax.optimization_barrier(jnp.max(score, axis=1, keepdims=True))
        lse = top + jnp.log(lax.optimization_barrier(jnp.sum(jnp.exp(score - top), axis=1, keepdims=True)))
        prob = jnp.exp(score - lse)
        weight = prob.astype(jnp.bfloat16)
        out = jnp.dot(weight, values, preferred_element_type=jnp.float32).astype(jnp.bfloat16)
        delta = lax.optimization_barrier(jnp.sum(cot.astype(jnp.float32) * out.astype(jnp.float32), axis=1, keepdims=True))
        grad_w = jnp.dot(cot, values.T, preferred_element_type=jnp.float32)
        dscore = (prob * (grad_w - delta) * factor).astype(jnp.bfloat16)
        dquery = jnp.dot(dscore, keys, preferred_element_type=jnp.float32)
        dkeys = jnp.dot(dscore.T, query, preferred_element_type=jnp.float32)
        dvalues = jnp.dot(weight.T, cot, preferred_element_type=jnp.float32)
        return (out, dquery, dkeys, dvalues)
    out_h, dq_h, dk_h, dv_h = lax.map(self_head, (by_head(prompt_qkv[0]), by_head(prompt_qkv[1]), by_head(prompt_qkv[2]), by_head(prompt_grad)))

    def unhead(x):
        return jnp.transpose(x, (1, 0, 2))
    pk32 = prompt_qkv[1].reshape(prompt_len, HEADS, HEAD_DIM).astype(jnp.float32)
    pv32 = prompt_qkv[2].reshape(prompt_len, HEADS, HEAD_DIM).astype(jnp.float32)
    position = jnp.arange(L, dtype=jnp.int32)
    valid = (position[None, :] < lengths[:, None]) & (keep_mask == 1)
    shape4 = (COMPS, L, HEADS, HEAD_DIM)

    def one(carry, items):
        dk_acc, dv_acc = carry
        query, keys, values, cot, okay = items
        cot = cot * okay[:, None, None].astype(jnp.bfloat16)
        q32 = query.astype(jnp.float32)
        k32 = keys.astype(jnp.float32)
        v32 = values.astype(jnp.float32)
        g32 = cot.astype(jnp.float32)
        far = jnp.einsum('lhe,phe->hlp', q32, pk32) * factor
        near = jnp.einsum('lhe,jhe->hlj', q32, k32) * factor
        near = jnp.where(okay[None, None, :], near, -jnp.inf)
        top = jnp.maximum(lax.optimization_barrier(jnp.max(far, axis=2, keepdims=True)), lax.optimization_barrier(jnp.max(near, axis=2, keepdims=True)))
        total = lax.optimization_barrier(jnp.sum(jnp.exp(far - top), axis=2, keepdims=True)) + lax.optimization_barrier(jnp.sum(jnp.exp(near - top), axis=2, keepdims=True))
        lse = top + jnp.log(total)
        prob_far = jnp.exp(far - lse)
        prob_near = jnp.exp(near - lse)
        wf32 = prob_far.astype(jnp.bfloat16).astype(jnp.float32)
        wn32 = prob_near.astype(jnp.bfloat16).astype(jnp.float32)
        out = (jnp.einsum('hlp,phe->lhe', wf32, pv32) + jnp.einsum('hlj,jhe->lhe', wn32, v32)).astype(jnp.bfloat16)
        delta = jnp.transpose(lax.optimization_barrier(jnp.sum(g32 * out.astype(jnp.float32), axis=2)))[:, :, None]
        grad_far = jnp.einsum('lhe,phe->hlp', g32, pv32)
        grad_near = jnp.einsum('lhe,jhe->hlj', g32, v32)
        ds_far = (prob_far * (grad_far - delta) * factor).astype(jnp.bfloat16).astype(jnp.float32)
        ds_near = (prob_near * (grad_near - delta) * factor).astype(jnp.bfloat16).astype(jnp.float32)
        dquery = jnp.einsum('hlp,phe->lhe', ds_far, pk32) + jnp.einsum('hlj,jhe->lhe', ds_near, k32)
        dkeys = jnp.einsum('hlj,lhe->jhe', ds_near, q32)
        dvalues = jnp.einsum('hlj,lhe->jhe', wn32, g32)
        dk_acc = dk_acc + jnp.einsum('hlp,lhe->phe', ds_far, q32)
        dv_acc = dv_acc + jnp.einsum('hlp,lhe->phe', wf32, g32)
        grads = jnp.stack([dquery, dkeys, dvalues]).astype(jnp.bfloat16)
        return ((dk_acc, dv_acc), (out, grads))
    start = (unhead(dk_h), unhead(dv_h))
    items = (comp_qkv[0].reshape(shape4), comp_qkv[1].reshape(shape4), comp_qkv[2].reshape(shape4), comp_grad.reshape(shape4), valid)
    (dk_all, dv_all), (comp_out, comp_grads) = lax.scan(one, start, items)
    prompt_out = unhead(out_h).reshape(prompt_len, D)
    prompt_dqkv = jnp.stack([unhead(dq_h), dk_all, dv_all]).astype(jnp.bfloat16).reshape(3, prompt_len, D)
    comp_out = comp_out.reshape(COMPS, L, D)
    comp_dqkv = jnp.transpose(comp_grads, (1, 0, 2, 3, 4)).reshape(3, COMPS, L, D)
    return (prompt_out, comp_out, prompt_dqkv, comp_dqkv)
```

```python
import math

import jax
import jax.numpy as jnp
from jax import lax
from jax.experimental import pallas as pl
from jax.experimental.pallas import tpu as pltpu
from jax.sharding import PartitionSpec as P

MESH = pl.DeviceIdType.MESH
BF16 = jnp.bfloat16
F32 = jnp.float32

HEAD_DIM = 128
FACTOR = 1.0 / math.sqrt(HEAD_DIM)
EXP2_FACTOR = FACTOR * math.log2(math.e)
MASKED = -1e30

SLOTS = 256
COMP_ROWS = 2 * SLOTS
OWN = 64
BLOCK = 2 * OWN
ROWS = COMP_ROWS + BLOCK
WIDTH = 256
PROMPT = 2048
CHUNK = 512
HALF = CHUNK // 2
STEP = 256
TOKENS = 32
PEERS = 16


def dot_nt(a, b):
    return lax.dot_general(a, b, (((1,), (1,)), ((), ())), preferred_element_type=F32)


def dot_nn(a, b):
    return lax.dot_general(a, b, (((1,), (0,)), ((), ())), preferred_element_type=F32)


def dot_tn(a, b):
    return lax.dot_general(a, b, (((0,), (0,)), ((), ())), preferred_element_type=F32)


def fold_rows(value, op):
    return op(value.reshape(value.shape[0] // 8, 8, value.shape[1]), axis=0)


def await_bytes(ref, sem):
    pltpu.make_async_copy(ref, ref, sem).wait()


def remote(src, dst, send_sem, recv_sem, device):
    copy = pltpu.make_async_remote_copy(
        src_ref=src,
        dst_ref=dst,
        send_sem=send_sem,
        recv_sem=recv_sem,
        device_id=device,
        device_id_type=MESH,
    )
    copy.start()


def kernel(
    pqkv, pgrad, cqkv, cgrad, lengths, mask,
    pout, cout, pdqkv, cdqkv,
    kv, x, v01, e, eb, en, enb, ot, dqt, gp, dl, dp, y_buf, ra, rb, rc, rd, za, zb, zc, zd,
    local_sem, pair_send, pair_recv, swap_send, swap_recv, ag_send, ag_recv,
    rs_send, rs_recv, back_send, back_recv, last_send, last_recv,
):
    seq = lax.axis_index("seq")
    head = lax.axis_index("head")
    y = seq // 8
    z = (seq // 2) % 4
    core = seq % 2
    other = 1 - core

    def at(yy, zz, cc):
        return ((yy * 4 + zz) * 2 + cc, head)

    partner = at(y, z, other)
    y_right, y_left, y_far = (y + 1) % 4, (y + 3) % 4, (y + 2) % 4
    z_right, z_left, z_far = (z + 1) % 4, (z + 3) % 4, (z + 2) % 4
    to_y_right, to_y_left = at(y_right, z, core), at(y_left, z, core)
    to_z_right, to_z_left = at(y, z_right, core), at(y, z_left, core)

    me = head * 2 + core

    def peer(step):
        there = (me + step) % PEERS
        return ((y * 4 + z) * 2 + there % 2, there // 2), there // 2, there % 2, there

    def rows(start, size):
        return pl.ds(pl.multiple_of(start, size), size)

    def lanes(index):
        return pl.ds(pl.multiple_of(index * WIDTH, WIDTH), WIDTH)

    own_rows = rows(seq * OWN, OWN)
    own_query = rows(COMP_ROWS + core * OWN, OWN)
    my_slots = rows(core * SLOTS + head * TOKENS, TOKENS)

    local = [
        pltpu.make_async_copy(pqkv.at[1:3, :, lanes(core)], kv.at[:, own_rows, :], local_sem.at[0]),
        pltpu.make_async_copy(pqkv.at[0, :, lanes(core)], x.at[0, own_query, :], local_sem.at[1]),
        pltpu.make_async_copy(pgrad.at[:, lanes(core)], x.at[3, own_query, :], local_sem.at[2]),
        pltpu.make_async_copy(
            cqkv.at[:, 0, :, lanes(me)], x.at[0:3, my_slots, :], local_sem.at[3]
        ),
        pltpu.make_async_copy(cgrad.at[0, :, lanes(me)], x.at[3, my_slots, :], local_sem.at[4]),
    ]
    for copy in local:
        copy.start()

    barrier = pltpu.get_barrier_semaphore()
    for step in range(1, PEERS):
        pl.semaphore_signal(barrier, inc=1, device_id=peer(step)[0], device_id_type=MESH)
    for device in (to_y_right, to_y_left, to_z_right, to_z_left):
        pl.semaphore_signal(barrier, inc=1, device_id=device, device_id_type=MESH)

    position = lax.broadcasted_iota(jnp.int32, (1, SLOTS), 1)
    valid = jnp.where((position < lengths[0]) & (mask[...] == 1), 1.0, 0.0)
    v01[core] = jnp.transpose(jnp.broadcast_to(valid, (HEAD_DIM, SLOTS)))

    pl.semaphore_wait(barrier, PEERS - 1 + 4)

    remote(
        pqkv.at[1:3, :, lanes(other)], kv.at[:, own_rows, :], pair_send.at[0], pair_recv.at[0], partner
    )
    remote(
        pqkv.at[0, :, lanes(other)], x.at[0, own_query, :], pair_send.at[1], pair_recv.at[1], partner
    )
    remote(
        pgrad.at[:, lanes(other)], x.at[3, own_query, :], pair_send.at[2], pair_recv.at[2], partner
    )
    remote(v01.at[core], v01.at[core], pair_send.at[3], pair_recv.at[3], partner)

    def swap(group):
        def body(step, carry):
            device, _, _, there = peer(step)
            if group == 0:
                src, dst = cqkv.at[0, 0, :, lanes(there)], x.at[0, my_slots, :]
            elif group == 1:
                src, dst = cqkv.at[1:3, 0, :, lanes(there)], x.at[1:3, my_slots, :]
            else:
                src, dst = cgrad.at[0, :, lanes(there)], x.at[3, my_slots, :]
            remote(src, dst, swap_send.at[group], swap_recv.at[group], device)
            return carry

        lax.fori_loop(1, PEERS, body, 0)

    def block_at(yy, zz):
        return (yy * 4 + zz) * BLOCK

    def ag(src_start, size, slot, device):
        part = kv.at[:, rows(src_start, size), :]
        remote(part, part, ag_send.at[slot], ag_recv.at[slot], device)

    def ag_wait(start, size, slot):
        await_bytes(kv.at[:, rows(start, size), :], ag_recv.at[slot])

    swap(0)
    local[0].wait()
    await_bytes(kv.at[:, own_rows, :], pair_recv.at[0])
    zs = (z, z_left, z_right, z_far)

    def y_send(j):
        ag(block_at(y, zs[j]), BLOCK, 4 + 4 * j, to_y_right)
        ag(block_at(y, zs[j]), BLOCK, 5 + 4 * j, to_y_left)

    def y_forward(j):
        ag_wait(block_at(y_left, zs[j]), BLOCK, 4 + 4 * j)
        ag(block_at(y_left, zs[j]), OWN, 6 + 4 * j, to_y_right)
        ag_wait(block_at(y_right, zs[j]), BLOCK, 5 + 4 * j)
        ag(block_at(y_right, zs[j]) + OWN, OWN, 7 + 4 * j, to_y_left)

    ag(block_at(y, z), BLOCK, 0, to_z_right)
    ag(block_at(y, z), BLOCK, 1, to_z_left)
    y_send(0)
    swap(2)
    swap(1)
    ag_wait(block_at(y, z_left), BLOCK, 0)
    ag(block_at(y, z_left), OWN, 2, to_z_right)
    ag_wait(block_at(y, z_right), BLOCK, 1)
    ag(block_at(y, z_right) + OWN, OWN, 3, to_z_left)
    y_send(1)
    y_send(2)
    y_forward(0)
    ag_wait(block_at(y, z_far), OWN, 2)
    ag_wait(block_at(y, z_far) + OWN, OWN, 3)
    y_send(3)
    y_forward(1)
    y_forward(2)
    y_forward(3)
    for j in range(4):
        ag_wait(block_at(y_far, zs[j]), OWN, 6 + 4 * j)
        ag_wait(block_at(y_far, zs[j]) + OWN, OWN, 7 + 4 * j)

    for copy in local[1:]:
        copy.wait()
    for slot in (1, 2):
        await_bytes(x.at[0, own_query, :], pair_recv.at[slot])
    await_bytes(v01.at[other], pair_recv.at[3])
    part = (PEERS - 1) * TOKENS
    await_bytes(x.at[0, 0:part, :], swap_recv.at[0])
    await_bytes(x.at[1:3, 0:part, :], swap_recv.at[1])
    await_bytes(x.at[3, 0:part, :], swap_recv.at[2])

    def head_lanes(h):
        return slice(h * HEAD_DIM, (h + 1) * HEAD_DIM)

    def slots_of(comp):
        return slice(comp * SLOTS, (comp + 1) * SLOTS)

    for h in range(2):
        hs = head_lanes(h)
        query = x[0, :, hs]

        def scores(step, top):
            keys = kv[0, rows(step * STEP, STEP), hs]
            score = dot_nt(keys, query)
            e[h, rows(step * STEP, STEP), :] = score
            return jnp.maximum(top, fold_rows(score, jnp.max))

        top = lax.fori_loop(0, PROMPT // STEP, scores, jnp.full((8, ROWS), MASKED, F32))
        near_top = []
        for comp in range(2):
            near = dot_nt(x[1, slots_of(comp), hs], x[0, slots_of(comp), hs])
            okay = v01[comp] > 0.5
            near = jnp.where(jnp.concatenate([okay, okay], axis=1), near, MASKED)
            en[h, slots_of(comp), :] = near
            near_top.append(fold_rows(near, jnp.max))
        near_top.append(jnp.full((8, BLOCK), MASKED, F32))
        top = jnp.maximum(top, jnp.concatenate(near_top, axis=1))
        top = jnp.max(top, axis=0, keepdims=True) * EXP2_FACTOR

        def exps(step, total):
            at_step = rows(step * STEP, STEP)
            grown = jnp.exp2(e[h, at_step, :] * EXP2_FACTOR - top)
            e[h, at_step, :] = grown
            eb[h, at_step, :] = grown.astype(BF16)
            return total + fold_rows(grown, jnp.sum)

        total = lax.fori_loop(0, PROMPT // STEP, exps, jnp.zeros((8, ROWS), F32))
        near_total = []
        for comp in range(2):
            cols = slots_of(comp)
            grown = jnp.exp2(en[h, cols, :] * EXP2_FACTOR - top[:, cols])
            en[h, cols, :] = grown
            enb[h, cols, :] = grown.astype(BF16)
            near_total.append(fold_rows(grown, jnp.sum))
        near_total.append(jnp.zeros((8, BLOCK), F32))
        total = total + jnp.concatenate(near_total, axis=1)
        inverse = 1.0 / jnp.sum(total, axis=0, keepdims=True)

        ot[...] = jnp.zeros_like(ot)

        def outs(step, carry):
            at_step = rows(step * STEP, STEP)
            ot[...] += dot_tn(kv[1, at_step, hs], eb[h, at_step, :])
            return carry

        lax.fori_loop(0, PROMPT // STEP, outs, 0)
        for comp in range(2):
            cols = slots_of(comp)
            ot[:, cols] += dot_tn(x[2, cols, hs], enb[h, cols, :])
        out = (ot[...] * inverse).astype(BF16).astype(F32)
        y_buf[3, :, hs] = jnp.transpose(out).astype(BF16)
        cot = [x[3, slots_of(comp), hs].astype(F32) * v01[comp] for comp in range(2)]
        cot = jnp.concatenate(cot + [x[3, COMP_ROWS:ROWS, hs].astype(F32)], axis=0)
        scaled = (jnp.transpose(cot) * inverse).astype(BF16).astype(F32)
        gp[:, hs] = jnp.transpose(scaled).astype(BF16)
        dl[h] = jnp.broadcast_to(jnp.sum(scaled * out, axis=0, keepdims=True), (8, ROWS))
        dqt[h] = jnp.zeros((HEAD_DIM, ROWS), F32)

    def back(group):
        def body(step, carry):
            device, there_head, there_core, _ = peer(step)
            slots = rows(there_core * SLOTS + there_head * TOKENS, TOKENS)
            if group == 0:
                src, dst = y_buf.at[3, slots, :], cout.at[0, :, lanes(me)]
            elif group == 1:
                src, dst = y_buf.at[1:3, slots, :], cdqkv.at[1:3, 0, :, lanes(me)]
            else:
                src, dst = y_buf.at[0, slots, :], cdqkv.at[0, 0, :, lanes(me)]
            remote(src, dst, back_send.at[group], back_recv.at[group], device)
            return carry

        lax.fori_loop(1, PEERS, body, 0)

    back(0)

    def gradients(yy):
        for h in range(2):
            hs = head_lanes(h)

            def body(step, carry):
                at_step = rows(yy * CHUNK + step * STEP, STEP)
                grad = dot_nt(kv[1, at_step, hs], gp[:, hs])
                ds = (e[h, at_step, :] * (grad - dl[h, 0:1, :])).astype(BF16)
                dp[0, at_step, hs] = dot_nn(ds, x[0, :, hs]).astype(BF16)
                dp[1, at_step, hs] = dot_nn(eb[h, at_step, :], gp[:, hs]).astype(BF16)
                dqt[h] += dot_tn(kv[0, at_step, hs], ds)
                return carry

            lax.fori_loop(0, CHUNK // STEP, body, 0)

    def rs(part, dst, slot, device):
        remote(part, dst, rs_send.at[slot], rs_recv.at[slot], device)

    def add_in(start, size, *arrived):
        width = min(size, 128)

        def body(step, carry):
            at_step = rows(start + step * width, width)
            there = rows(step * width, width)
            total = dp[:, at_step, :].astype(F32)
            for ref in arrived:
                total = total + ref[:, there, :].astype(F32)
            dp[:, at_step, :] = total.astype(BF16)
            return carry

        lax.fori_loop(0, size // width, body, 0)

    def dp_rows(start, size):
        return dp.at[:, rows(start, size), :]

    gradients(y_far)
    rs(dp_rows(y_far * CHUNK, HALF), ra, 0, to_y_right)
    rs(dp_rows(y_far * CHUNK + HALF, HALF), rb, 1, to_y_left)

    for h in range(2):
        hs = head_lanes(h)
        for comp in range(2):
            cols = slots_of(comp)
            grad = dot_nt(x[2, cols, hs], gp[cols, hs])
            ds = (en[h, cols, :] * (grad - dl[h, 0:1, cols])).astype(BF16)
            y_buf[1, cols, hs] = (dot_nn(ds, x[0, cols, hs]) * FACTOR).astype(BF16)
            y_buf[2, cols, hs] = dot_nn(enb[h, cols, :], gp[cols, hs]).astype(BF16)
            dqt[h, :, cols] += dot_tn(x[1, cols, hs], ds)
    back(1)

    gradients(y_right)
    rs(dp_rows(y_right * CHUNK + HALF, HALF), rc.at[:, HALF:CHUNK, :], 3, to_y_right)
    await_bytes(ra, rs_recv.at[0])
    add_in(y_right * CHUNK, HALF, ra)
    rs(dp_rows(y_right * CHUNK, HALF), rc.at[:, 0:HALF, :], 2, to_y_right)
    gradients(y_left)
    rs(dp_rows(y_left * CHUNK, HALF), rd.at[:, 0:HALF, :], 4, to_y_left)
    await_bytes(rb, rs_recv.at[1])
    add_in(y_left * CHUNK + HALF, HALF, rb)
    rs(dp_rows(y_left * CHUNK + HALF, HALF), rd.at[:, HALF:CHUNK, :], 5, to_y_left)
    gradients(y)

    for h in range(2):
        y_buf[0, :, head_lanes(h)] = jnp.transpose(dqt[h] * FACTOR).astype(BF16)
    back(2)

    partner_query = rows(COMP_ROWS + other * OWN, OWN)
    my_half = lanes(core)
    remote(
        y_buf.at[3, partner_query, :], pout.at[:, my_half], last_send.at[0], last_recv.at[0], partner
    )
    remote(
        y_buf.at[0, partner_query, :], pdqkv.at[0, :, my_half], last_send.at[1], last_recv.at[1], partner
    )
    final = [
        pltpu.make_async_copy(y_buf.at[3, own_query, :], pout.at[:, my_half], local_sem.at[0]),
        pltpu.make_async_copy(y_buf.at[0, own_query, :], pdqkv.at[0, :, my_half], local_sem.at[1]),
        pltpu.make_async_copy(
            y_buf.at[0:3, my_slots, :], cdqkv.at[:, 0, :, lanes(me)], local_sem.at[2]
        ),
        pltpu.make_async_copy(y_buf.at[3, my_slots, :], cout.at[0, :, lanes(me)], local_sem.at[3]),
    ]
    for copy in final:
        copy.start()

    await_bytes(rc.at[:, HALF:CHUNK, :], rs_recv.at[3])
    await_bytes(rd.at[:, 0:HALF, :], rs_recv.at[4])
    await_bytes(rc.at[:, 0:HALF, :], rs_recv.at[2])
    await_bytes(rd.at[:, HALF:CHUNK, :], rs_recv.at[5])
    add_in(y * CHUNK, CHUNK, rc, rd)

    rs(dp_rows(block_at(y, z_far), OWN), za, 6, to_z_right)
    rs(dp_rows(block_at(y, z_far) + OWN, OWN), zb, 7, to_z_left)
    await_bytes(za, rs_recv.at[6])
    add_in(block_at(y, z_right), OWN, za)
    rs(dp_rows(block_at(y, z_right), BLOCK), zc, 8, to_z_right)
    await_bytes(zb, rs_recv.at[7])
    add_in(block_at(y, z_left) + OWN, OWN, zb)
    rs(dp_rows(block_at(y, z_left), BLOCK), zd, 9, to_z_left)
    await_bytes(zc, rs_recv.at[8])
    await_bytes(zd, rs_recv.at[9])
    mine = rows(block_at(y, z), BLOCK)
    total = dp[:, mine, :].astype(F32) + zc[...].astype(F32) + zd[...].astype(F32)
    dp[0, mine, :] = (total[0] * FACTOR).astype(BF16)
    dp[1, mine, :] = total[1].astype(BF16)
    partner_rows = rows(block_at(y, z) + other * OWN, OWN)
    remote(
        dp.at[:, partner_rows, :], pdqkv.at[1:3, :, my_half], last_send.at[2], last_recv.at[2], partner
    )
    last = pltpu.make_async_copy(dp.at[:, own_rows, :], pdqkv.at[1:3, :, my_half], local_sem.at[4])
    last.start()

    other_half = lanes(other)
    for slot in range(20):
        size = BLOCK if slot < 2 or (slot >= 4 and slot % 4 < 2) else OWN
        await_bytes(kv.at[:, 0:size, :], ag_send.at[slot])
    for slot, size in enumerate((HALF,) * 6 + (OWN, OWN, BLOCK, BLOCK)):
        await_bytes(dp.at[:, 0:size, :], rs_send.at[slot])
    await_bytes(kv.at[:, own_rows, :], pair_send.at[0])
    for slot in (1, 2):
        await_bytes(x.at[0, own_query, :], pair_send.at[slot])
    await_bytes(v01.at[core], pair_send.at[3])
    for group, ref in enumerate((x.at[0, 0:part, :], x.at[1:3, 0:part, :], x.at[3, 0:part, :])):
        await_bytes(ref, swap_send.at[group])
    for group, ref in enumerate(
        (y_buf.at[3, 0:part, :], y_buf.at[1:3, 0:part, :], y_buf.at[0, 0:part, :])
    ):
        await_bytes(ref, back_send.at[group])
        await_bytes(ref, back_recv.at[group])
    await_bytes(pout.at[:, other_half], last_send.at[0])
    await_bytes(pout.at[:, other_half], last_recv.at[0])
    await_bytes(pdqkv.at[0, :, other_half], last_send.at[1])
    await_bytes(pdqkv.at[0, :, other_half], last_recv.at[1])
    await_bytes(pdqkv.at[1:3, :, other_half], last_send.at[2])
    await_bytes(pdqkv.at[1:3, :, other_half], last_recv.at[2])
    for copy in final:
        copy.wait()
    last.wait()


def local(prompt_qkv, prompt_grad, comp_qkv, comp_grad, lengths, keep_mask):
    hbm = pl.BlockSpec(memory_space=pl.ANY)
    vmem = pltpu.VMEM
    dma = pltpu.SemaphoreType.DMA
    return pl.pallas_call(
        kernel,
        out_shape=(
            jax.ShapeDtypeStruct((OWN, 2 * WIDTH), BF16),
            jax.ShapeDtypeStruct((1, TOKENS, PEERS * WIDTH), BF16),
            jax.ShapeDtypeStruct((3, OWN, 2 * WIDTH), BF16),
            jax.ShapeDtypeStruct((3, 1, TOKENS, PEERS * WIDTH), BF16),
        ),
        in_specs=[
            hbm,
            hbm,
            hbm,
            hbm,
            pl.BlockSpec(memory_space=pltpu.SMEM),
            pl.BlockSpec(memory_space=pltpu.VMEM),
        ],
        out_specs=(hbm, hbm, hbm, hbm),
        scratch_shapes=[
            vmem((2, PROMPT, WIDTH), BF16),
            vmem((4, ROWS, WIDTH), BF16),
            vmem((2, SLOTS, HEAD_DIM), F32),
            vmem((2, PROMPT, ROWS), F32),
            vmem((2, PROMPT, ROWS), BF16),
            vmem((2, COMP_ROWS, SLOTS), F32),
            vmem((2, COMP_ROWS, SLOTS), BF16),
            vmem((HEAD_DIM, ROWS), F32),
            vmem((2, HEAD_DIM, ROWS), F32),
            vmem((ROWS, WIDTH), BF16),
            vmem((2, 8, ROWS), F32),
            vmem((2, PROMPT, WIDTH), BF16),
            vmem((4, ROWS, WIDTH), BF16),
            vmem((2, HALF, WIDTH), BF16),
            vmem((2, HALF, WIDTH), BF16),
            vmem((2, CHUNK, WIDTH), BF16),
            vmem((2, CHUNK, WIDTH), BF16),
            vmem((2, OWN, WIDTH), BF16),
            vmem((2, OWN, WIDTH), BF16),
            vmem((2, BLOCK, WIDTH), BF16),
            vmem((2, BLOCK, WIDTH), BF16),
            dma((5,)),
            dma((4,)),
            dma((4,)),
            dma((3,)),
            dma((3,)),
            dma((20,)),
            dma((20,)),
            dma((10,)),
            dma((10,)),
            dma((3,)),
            dma((3,)),
            dma((3,)),
            dma((3,)),
        ],
        compiler_params=pltpu.CompilerParams(
            collective_id=0, has_side_effects=True, vmem_limit_bytes=56 * 1024 * 1024
        ),
        name="attention",
    )(prompt_qkv, prompt_grad, comp_qkv, comp_grad, lengths, keep_mask)


def solution(mesh):
    in_specs = (
        P(None, "seq", "head"),
        P("seq", "head"),
        P(None, "seq", "head", None),
        P("seq", "head", None),
        P("seq"),
        P("seq", None),
    )
    out_specs = (
        P("seq", "head"),
        P("seq", "head", None),
        P(None, "seq", "head"),
        P(None, "seq", "head", None),
    )
    return jax.shard_map(local, mesh=mesh, in_specs=in_specs, out_specs=out_specs, check_vma=False)
```

```python
import math

import jax
import jax.numpy as jnp
from jax import lax
from jax.experimental import pallas as pl
from jax.experimental.pallas import tpu as pltpu
from jax.sharding import PartitionSpec as P

MESH = pl.DeviceIdType.MESH
BF16 = jnp.bfloat16
F32 = jnp.float32

HEAD_DIM = 128
FACTOR = 1.0 / math.sqrt(HEAD_DIM)
EXP2_FACTOR = FACTOR * math.log2(math.e)
MASKED = -1e30

SLOTS = 256
COMP_ROWS = 2 * SLOTS
OWN = 64
BLOCK = 2 * OWN
ROWS = COMP_ROWS + BLOCK
WIDTH = 256
PROMPT = 2048
CHUNK = 512
STEP = 256
TOKENS = 32
PEERS = 16


def dot_nt(a, b):
    return lax.dot_general(a, b, (((1,), (1,)), ((), ())), preferred_element_type=F32)


def dot_nn(a, b):
    return lax.dot_general(a, b, (((1,), (0,)), ((), ())), preferred_element_type=F32)


def dot_tn(a, b):
    return lax.dot_general(a, b, (((0,), (0,)), ((), ())), preferred_element_type=F32)


def fold_rows(value, op):
    return op(value.reshape(value.shape[0] // 8, 8, value.shape[1]), axis=0)


def await_bytes(ref, sem):
    pltpu.make_async_copy(ref, ref, sem).wait()


def remote(src, dst, send_sem, recv_sem, device):
    copy = pltpu.make_async_remote_copy(
        src_ref=src,
        dst_ref=dst,
        send_sem=send_sem,
        recv_sem=recv_sem,
        device_id=device,
        device_id_type=MESH,
    )
    copy.start()


def kernel(
    pqkv, pgrad, cqkv, cgrad, lengths, mask,
    pout, cout, pdqkv, cdqkv,
    kv, x, v01, e, eb, en, enb, dsb, tops, ot, gp, dl, dp, y_buf, ra, rb, rc, rd, za, zb, zc, zd,
    local_sem, pair_send, pair_recv, swap_send, swap_recv, ag_send, ag_recv,
    rs_send, rs_recv, back_send, back_recv, last_send, last_recv,
):
    seq = lax.axis_index("seq")
    head = lax.axis_index("head")
    y = seq // 8
    z = (seq // 2) % 4
    core = seq % 2
    other = 1 - core

    def at(yy, zz, cc):
        return ((yy * 4 + zz) * 2 + cc, head)

    partner = at(y, z, other)
    y_right, y_left, y_far = (y + 1) % 4, (y + 3) % 4, (y + 2) % 4
    z_right, z_left, z_far = (z + 1) % 4, (z + 3) % 4, (z + 2) % 4
    to_y_right, to_y_left = at(y_right, z, core), at(y_left, z, core)
    to_z_right, to_z_left = at(y, z_right, core), at(y, z_left, core)

    me = head * 2 + core

    def peer(step):
        there = (me + step) % PEERS
        return ((y * 4 + z) * 2 + there % 2, there // 2), there // 2, there % 2, there

    def rows(start, size):
        return pl.ds(pl.multiple_of(start, size), size)

    def lanes(index):
        return pl.ds(pl.multiple_of(index * WIDTH, WIDTH), WIDTH)

    own_rows = rows(seq * OWN, OWN)
    own_query = rows(COMP_ROWS + core * OWN, OWN)
    my_slots = rows(core * SLOTS + head * TOKENS, TOKENS)

    local = [
        pltpu.make_async_copy(pqkv.at[1:3, :, lanes(core)], kv.at[:, own_rows, :], local_sem.at[0]),
        pltpu.make_async_copy(pqkv.at[0, :, lanes(core)], x.at[0, own_query, :], local_sem.at[1]),
        pltpu.make_async_copy(pgrad.at[:, lanes(core)], x.at[3, own_query, :], local_sem.at[2]),
        pltpu.make_async_copy(
            cqkv.at[:, 0, :, lanes(me)], x.at[0:3, my_slots, :], local_sem.at[3]
        ),
        pltpu.make_async_copy(cgrad.at[0, :, lanes(me)], x.at[3, my_slots, :], local_sem.at[4]),
    ]
    for copy in local:
        copy.start()

    barrier = pltpu.get_barrier_semaphore()
    for device in (to_y_right, to_y_left, to_z_right, to_z_left):
        pl.semaphore_signal(barrier, inc=1, device_id=device, device_id_type=MESH)
    for step in range(1, PEERS):
        pl.semaphore_signal(barrier, inc=1, device_id=peer(step)[0], device_id_type=MESH)

    position = lax.broadcasted_iota(jnp.int32, (1, SLOTS), 1)
    valid = jnp.where((position < lengths[0]) & (mask[...] == 1), 1.0, 0.0)
    v01[core] = jnp.transpose(jnp.broadcast_to(valid, (HEAD_DIM, SLOTS)))

    pl.semaphore_wait(barrier, PEERS - 1 + 4)

    for part in range(2):
        remote(
            pqkv.at[1 + part, :, lanes(other)], kv.at[part, own_rows, :],
            pair_send.at[part], pair_recv.at[part], partner,
        )

    def swap(group):
        def body(step, carry):
            device, _, _, there = peer(step)
            if group < 3:
                src = cqkv.at[group, 0, :, lanes(there)]
            else:
                src = cgrad.at[0, :, lanes(there)]
            remote(src, x.at[group, my_slots, :], swap_send.at[group], swap_recv.at[group], device)
            return carry

        lax.fori_loop(1, PEERS, body, 0)

    others = (PEERS - 1) * TOKENS

    def await_swap(group):
        await_bytes(x.at[group, 0:others, :], swap_recv.at[group])

    def block_at(yy, zz):
        return (yy * 4 + zz) * BLOCK

    def ag(t, start, size, slot, device):
        part = kv.at[t, rows(start, size), :]
        remote(part, part, ag_send.at[t, slot], ag_recv.at[t, slot], device)

    def ag_wait(t, start, size, slot):
        await_bytes(kv.at[t, rows(start, size), :], ag_recv.at[t, slot])

    zs = (z, z_left, z_right, z_far)

    def y_send(t, j):
        ag(t, block_at(y, zs[j]), BLOCK, 4 + 4 * j, to_y_right)
        ag(t, block_at(y, zs[j]), BLOCK, 5 + 4 * j, to_y_left)

    def y_forward(t, j):
        ag_wait(t, block_at(y_left, zs[j]), BLOCK, 4 + 4 * j)
        ag(t, block_at(y_left, zs[j]), OWN, 6 + 4 * j, to_y_right)
        ag_wait(t, block_at(y_right, zs[j]), BLOCK, 5 + 4 * j)
        ag(t, block_at(y_right, zs[j]) + OWN, OWN, 7 + 4 * j, to_y_left)

    def z_forward(t):
        ag_wait(t, block_at(y, z_left), BLOCK, 0)
        ag(t, block_at(y, z_left), OWN, 2, to_z_right)
        ag_wait(t, block_at(y, z_right), BLOCK, 1)
        ag(t, block_at(y, z_right) + OWN, OWN, 3, to_z_left)
        y_send(t, 1)
        y_send(t, 2)

    def z_end(t):
        ag_wait(t, block_at(y, z_far), OWN, 2)
        ag_wait(t, block_at(y, z_far) + OWN, OWN, 3)
        y_send(t, 3)

    def y_end(t):
        for j in range(4):
            ag_wait(t, block_at(y_far, zs[j]), OWN, 6 + 4 * j)
            ag_wait(t, block_at(y_far, zs[j]) + OWN, OWN, 7 + 4 * j)

    def head_lanes(h):
        return slice(h * HEAD_DIM, (h + 1) * HEAD_DIM)

    def slots_of(comp):
        return slice(comp * SLOTS, (comp + 1) * SLOTS)

    def scores(yy):
        def body(step, carry):
            at_step = rows(yy * CHUNK + step * STEP, STEP)
            for h in range(2):
                score = dot_nt(kv[0, at_step, head_lanes(h)], x[0, :, head_lanes(h)])
                e[h, at_step, :] = score
                tops[h] = jnp.maximum(tops[h], fold_rows(score, jnp.max))
            return carry

        lax.fori_loop(0, CHUNK // STEP, body, 0)

    swap(0)
    remote(
        pqkv.at[0, :, lanes(other)], x.at[0, own_query, :], pair_send.at[2], pair_recv.at[2], partner
    )
    remote(
        pgrad.at[:, lanes(other)], x.at[3, own_query, :], pair_send.at[3], pair_recv.at[3], partner
    )
    remote(v01.at[core], v01.at[core], pair_send.at[4], pair_recv.at[4], partner)
    local[0].wait()
    for t in range(2):
        await_bytes(kv.at[t, own_rows, :], pair_recv.at[t])
        ag(t, block_at(y, z), BLOCK, 0, to_z_right)
        ag(t, block_at(y, z), BLOCK, 1, to_z_left)
        y_send(t, 0)
    tops[...] = jnp.full(tops.shape, MASKED, F32)
    z_forward(0)
    y_forward(0, 0)
    z_forward(1)
    swap(1)
    y_forward(1, 0)
    z_end(0)
    y_forward(0, 1)
    y_forward(0, 2)
    z_end(1)
    swap(3)
    swap(2)
    for copy in local[1:]:
        copy.wait()
    for slot in (2, 3):
        await_bytes(x.at[0, own_query, :], pair_recv.at[slot])
    await_bytes(v01.at[other], pair_recv.at[4])
    await_swap(0)
    scores(y)
    y_forward(1, 1)
    y_forward(1, 2)
    y_forward(0, 3)
    scores(y_right)
    y_forward(1, 3)
    scores(y_left)
    y_end(0)
    scores(y_far)

    await_swap(1)
    inverses = []
    for h in range(2):
        hs = head_lanes(h)
        near_top = []
        for comp in range(2):
            near = dot_nt(x[1, slots_of(comp), hs], x[0, slots_of(comp), hs])
            okay = v01[comp] > 0.5
            near = jnp.where(jnp.concatenate([okay, okay], axis=1), near, MASKED)
            en[h, slots_of(comp), :] = near
            near_top.append(fold_rows(near, jnp.max))
        near_top.append(jnp.full((8, BLOCK), MASKED, F32))
        top = jnp.maximum(tops[h], jnp.concatenate(near_top, axis=1))
        top = jnp.max(top, axis=0, keepdims=True) * EXP2_FACTOR

        def exps(step, total):
            at_step = rows(step * STEP, STEP)
            grown = jnp.exp2(e[h, at_step, :] * EXP2_FACTOR - top)
            e[h, at_step, :] = grown
            eb[h, at_step, :] = grown.astype(BF16)
            return total + fold_rows(grown, jnp.sum)

        total = lax.fori_loop(0, PROMPT // STEP, exps, jnp.zeros((8, ROWS), F32))
        near_total = []
        for comp in range(2):
            cols = slots_of(comp)
            grown = jnp.exp2(en[h, cols, :] * EXP2_FACTOR - top[:, cols])
            en[h, cols, :] = grown
            enb[h, cols, :] = grown.astype(BF16)
            near_total.append(fold_rows(grown, jnp.sum))
        near_total.append(jnp.zeros((8, BLOCK), F32))
        total = total + jnp.concatenate(near_total, axis=1)
        inverses.append(1.0 / jnp.sum(total, axis=0, keepdims=True))

    ot[...] = jnp.zeros_like(ot)

    def outs(j, carry):
        yy = (y + j + j // 2 - 2 * (j // 3)) % 4

        @pl.when(j == 3)
        def _():
            y_end(1)

        for h in range(2):
            at_step = rows(yy * CHUNK, CHUNK)
            ot[h] += dot_tn(kv[1, at_step, head_lanes(h)], eb[h, at_step, :])
        return carry

    lax.fori_loop(0, 4, outs, 0)
    await_swap(2)
    await_swap(3)
    for h in range(2):
        hs = head_lanes(h)
        inverse = inverses[h]
        for comp in range(2):
            cols = slots_of(comp)
            ot[h, :, cols] += dot_tn(x[2, cols, hs], enb[h, cols, :])
        out = (ot[h] * inverse).astype(BF16).astype(F32)
        y_buf[3, :, hs] = jnp.transpose(out).astype(BF16)
        cot = [x[3, slots_of(comp), hs].astype(F32) * v01[comp] for comp in range(2)]
        cot = jnp.concatenate(cot + [x[3, COMP_ROWS:ROWS, hs].astype(F32)], axis=0)
        scaled = (jnp.transpose(cot) * inverse).astype(BF16).astype(F32)
        gp[:, hs] = jnp.transpose(scaled).astype(BF16)
        dl[h] = jnp.broadcast_to(jnp.sum(scaled * out, axis=0, keepdims=True), (8, ROWS))

    def back(group):
        def body(step, carry):
            device, there_head, there_core, _ = peer(step)
            slots = rows(there_core * SLOTS + there_head * TOKENS, TOKENS)
            if group == 0:
                src, dst = y_buf.at[3, slots, :], cout.at[0, :, lanes(me)]
            elif group == 1:
                src, dst = y_buf.at[1:3, slots, :], cdqkv.at[1:3, 0, :, lanes(me)]
            else:
                src, dst = y_buf.at[0, slots, :], cdqkv.at[0, 0, :, lanes(me)]
            remote(src, dst, back_send.at[group], back_recv.at[group], device)
            return carry

        lax.fori_loop(1, PEERS, body, 0)

    def ordered(place, j):
        return (place + 10 - j - j // 2 + 2 * (j // 3)) % 4

    def gradients(start):
        at_step = rows(start, BLOCK)
        for h in range(2):
            hs = head_lanes(h)
            grad = dot_nt(kv[1, at_step, hs], gp[:, hs])
            ds = (e[h, at_step, :] * (grad - dl[h, 0:1, :])).astype(BF16)
            dsb[h, at_step, :] = ds
            dp[0, at_step, hs] = dot_nn(ds, x[0, :, hs]).astype(BF16)
            dp[1, at_step, hs] = dot_nn(eb[h, at_step, :], gp[:, hs]).astype(BF16)

    def dp_rows(start, size):
        return dp.at[:, rows(start, size), :]

    def rs(part, dst, slot, device):
        remote(part, dst, rs_send.at[slot], rs_recv.at[slot], device)

    def add_half(start, arrived):
        at_half = rows(start, OWN)
        dp[:, at_half, :] = (dp[:, at_half, :].astype(F32) + arrived.astype(F32)).astype(BF16)

    z_order = (z_far, z_right, z_left, z)

    def y_first(i):
        far = block_at(y_far, z_order[i])
        rs(dp_rows(far, OWN), ra.at[i], 6 * i, to_y_right)
        rs(dp_rows(far + OWN, OWN), rb.at[i], 6 * i + 1, to_y_left)

    def y_second(i):
        right, left = block_at(y_right, z_order[i]), block_at(y_left, z_order[i])
        rs(dp_rows(right + OWN, OWN), rc.at[i, :, OWN:BLOCK, :], 6 * i + 2, to_y_right)
        rs(dp_rows(left, OWN), rd.at[i, :, 0:OWN, :], 6 * i + 3, to_y_left)

    def y_third(i):
        right, left = block_at(y_right, z_order[i]), block_at(y_left, z_order[i])
        await_bytes(ra.at[i], rs_recv.at[6 * i])
        add_half(right, ra[i])
        rs(dp_rows(right, OWN), rc.at[i, :, 0:OWN, :], 6 * i + 4, to_y_right)
        await_bytes(rb.at[i], rs_recv.at[6 * i + 1])
        add_half(left + OWN, rb[i])
        rs(dp_rows(left + OWN, OWN), rd.at[i, :, OWN:BLOCK, :], 6 * i + 5, to_y_left)

    def y_total(i):
        for slot in (2, 4):
            await_bytes(rc.at[i, :, 0:OWN, :], rs_recv.at[6 * i + slot])
        for slot in (3, 5):
            await_bytes(rd.at[i, :, 0:OWN, :], rs_recv.at[6 * i + slot])
        own = dp[:, rows(block_at(y, z_order[i]), BLOCK), :]
        return own.astype(F32) + rc[i].astype(F32) + rd[i].astype(F32)

    def z_first():
        dp[:, rows(block_at(y, z_far), BLOCK), :] = y_total(0).astype(BF16)
        rs(dp_rows(block_at(y, z_far), OWN), za, 24, to_z_right)
        rs(dp_rows(block_at(y, z_far) + OWN, OWN), zb, 25, to_z_left)

    def near_gradients():
        for h in range(2):
            hs = head_lanes(h)
            for comp in range(2):
                cols = slots_of(comp)
                grad = dot_nt(x[2, cols, hs], gp[cols, hs])
                ds = (en[h, cols, :] * (grad - dl[h, 0:1, cols])).astype(BF16)
                y_buf[1, cols, hs] = (dot_nn(ds, x[0, cols, hs]) * FACTOR).astype(BF16)
                y_buf[2, cols, hs] = dot_nn(enb[h, cols, :], gp[cols, hs]).astype(BF16)
                ot[h, :, cols] = dot_tn(x[1, cols, hs], ds)
            ot[h, :, COMP_ROWS:ROWS] = jnp.zeros((HEAD_DIM, BLOCK), F32)
        back(1)

    events = {}
    for i in range(4):
        events.setdefault(4 * i, []).append(lambda i=i: y_first(i))
        events.setdefault(4 * i + 2, []).append(lambda i=i: y_second(i))
        if i < 3:
            events.setdefault(4 * i + 6, []).append(lambda i=i: y_third(i))
    events[0].append(near_gradients)
    events.setdefault(13, []).append(z_first)

    back(0)

    def gradient_step(step, carry):
        gradients(block_at(ordered(y, step % 4), ordered(z, step // 4)))
        for when, todo in sorted(events.items()):

            @pl.when(step == when)
            def _():
                for event in todo:
                    event()

        return carry

    lax.fori_loop(0, 16, gradient_step, 0)
    y_third(3)

    def query_gradients(step, carry):
        at_step = rows(step * CHUNK, CHUNK)
        for h in range(2):
            ot[h] += dot_tn(kv[0, at_step, head_lanes(h)], dsb[h, at_step, :])
        return carry

    lax.fori_loop(0, 4, query_gradients, 0)
    for h in range(2):
        y_buf[0, :, head_lanes(h)] = jnp.transpose(ot[h] * FACTOR).astype(BF16)
    back(2)

    right_block = block_at(y, z_right)
    dp[:, rows(right_block, BLOCK), :] = y_total(1).astype(BF16)
    await_bytes(za, rs_recv.at[24])
    add_half(right_block, za[...])
    rs(dp_rows(right_block, BLOCK), zc, 26, to_z_right)
    left_block = block_at(y, z_left)
    dp[:, rows(left_block, BLOCK), :] = y_total(2).astype(BF16)
    await_bytes(zb, rs_recv.at[25])
    add_half(left_block + OWN, zb[...])
    rs(dp_rows(left_block, BLOCK), zd, 27, to_z_left)

    partner_query = rows(COMP_ROWS + other * OWN, OWN)
    my_half = lanes(core)
    remote(
        y_buf.at[3, partner_query, :], pout.at[:, my_half], last_send.at[0], last_recv.at[0], partner
    )
    remote(
        y_buf.at[0, partner_query, :], pdqkv.at[0, :, my_half], last_send.at[1], last_recv.at[1], partner
    )
    final = [
        pltpu.make_async_copy(y_buf.at[3, own_query, :], pout.at[:, my_half], local_sem.at[0]),
        pltpu.make_async_copy(y_buf.at[0, own_query, :], pdqkv.at[0, :, my_half], local_sem.at[1]),
        pltpu.make_async_copy(
            y_buf.at[0:3, my_slots, :], cdqkv.at[:, 0, :, lanes(me)], local_sem.at[2]
        ),
        pltpu.make_async_copy(y_buf.at[3, my_slots, :], cout.at[0, :, lanes(me)], local_sem.at[3]),
    ]
    for copy in final:
        copy.start()

    total = y_total(3)
    await_bytes(zc, rs_recv.at[26])
    await_bytes(zd, rs_recv.at[27])
    total = total + zc[...].astype(F32) + zd[...].astype(F32)
    mine = rows(block_at(y, z), BLOCK)
    dp[0, mine, :] = (total[0] * FACTOR).astype(BF16)
    dp[1, mine, :] = total[1].astype(BF16)
    partner_rows = rows(block_at(y, z) + other * OWN, OWN)
    remote(
        dp.at[:, partner_rows, :], pdqkv.at[1:3, :, my_half], last_send.at[2], last_recv.at[2], partner
    )
    last = pltpu.make_async_copy(dp.at[:, own_rows, :], pdqkv.at[1:3, :, my_half], local_sem.at[4])
    last.start()

    other_half = lanes(other)
    for t in range(2):
        for slot in range(20):
            size = BLOCK if slot < 2 or (slot >= 4 and slot % 4 < 2) else OWN
            await_bytes(kv.at[t, 0:size, :], ag_send.at[t, slot])
    for slot in range(28):
        await_bytes(dp.at[:, 0 : OWN if slot < 26 else BLOCK, :], rs_send.at[slot])
    for slot in range(4):
        await_bytes(x.at[0, own_query, :], pair_send.at[slot])
    await_bytes(v01.at[core], pair_send.at[4])
    for group in range(4):
        await_bytes(x.at[group, 0:others, :], swap_send.at[group])
    for group, ref in enumerate(
        (y_buf.at[3, 0:others, :], y_buf.at[1:3, 0:others, :], y_buf.at[0, 0:others, :])
    ):
        await_bytes(ref, back_send.at[group])
        await_bytes(ref, back_recv.at[group])
    await_bytes(pout.at[:, other_half], last_send.at[0])
    await_bytes(pout.at[:, other_half], last_recv.at[0])
    await_bytes(pdqkv.at[0, :, other_half], last_send.at[1])
    await_bytes(pdqkv.at[0, :, other_half], last_recv.at[1])
    await_bytes(pdqkv.at[1:3, :, other_half], last_send.at[2])
    await_bytes(pdqkv.at[1:3, :, other_half], last_recv.at[2])
    for copy in final:
        copy.wait()
    last.wait()


def place(*refs):
    sources, targets, held, sem = refs[:4], refs[4:8], refs[8:12], refs[12]
    into = [pltpu.make_async_copy(sources[i], held[i], sem.at[0, i]) for i in range(4)]
    out = [pltpu.make_async_copy(held[i], targets[i], sem.at[1, i]) for i in range(4)]
    for copy in into:
        copy.start()
    for i in range(4):
        into[i].wait()
        out[i].start()
    for copy in out:
        copy.wait()


def local(prompt_qkv, prompt_grad, comp_qkv, comp_grad, lengths, keep_mask):
    hbm = pl.BlockSpec(memory_space=pl.ANY)
    vmem = pltpu.VMEM
    dma = pltpu.SemaphoreType.DMA
    results = pl.pallas_call(
        kernel,
        out_shape=(
            jax.ShapeDtypeStruct((OWN, 2 * WIDTH), BF16),
            jax.ShapeDtypeStruct((1, TOKENS, PEERS * WIDTH), BF16),
            jax.ShapeDtypeStruct((3, OWN, 2 * WIDTH), BF16),
            jax.ShapeDtypeStruct((3, 1, TOKENS, PEERS * WIDTH), BF16),
        ),
        in_specs=[
            hbm,
            hbm,
            hbm,
            hbm,
            pl.BlockSpec(memory_space=pltpu.SMEM),
            pl.BlockSpec(memory_space=pltpu.VMEM),
        ],
        out_specs=(hbm, hbm, hbm, hbm),
        scratch_shapes=[
            vmem((2, PROMPT, WIDTH), BF16),
            vmem((4, ROWS, WIDTH), BF16),
            vmem((2, SLOTS, HEAD_DIM), F32),
            vmem((2, PROMPT, ROWS), F32),
            vmem((2, PROMPT, ROWS), BF16),
            vmem((2, COMP_ROWS, SLOTS), F32),
            vmem((2, COMP_ROWS, SLOTS), BF16),
            vmem((2, PROMPT, ROWS), BF16),
            vmem((2, 8, ROWS), F32),
            vmem((2, HEAD_DIM, ROWS), F32),
            vmem((ROWS, WIDTH), BF16),
            vmem((2, 8, ROWS), F32),
            vmem((2, PROMPT, WIDTH), BF16),
            vmem((4, ROWS, WIDTH), BF16),
            vmem((4, 2, OWN, WIDTH), BF16),
            vmem((4, 2, OWN, WIDTH), BF16),
            vmem((4, 2, BLOCK, WIDTH), BF16),
            vmem((4, 2, BLOCK, WIDTH), BF16),
            vmem((2, OWN, WIDTH), BF16),
            vmem((2, OWN, WIDTH), BF16),
            vmem((2, BLOCK, WIDTH), BF16),
            vmem((2, BLOCK, WIDTH), BF16),
            dma((5,)),
            dma((5,)),
            dma((5,)),
            dma((4,)),
            dma((4,)),
            dma((2, 20)),
            dma((2, 20)),
            dma((28,)),
            dma((28,)),
            dma((3,)),
            dma((3,)),
            dma((3,)),
            dma((3,)),
        ],
        compiler_params=pltpu.CompilerParams(
            collective_id=0, has_side_effects=True, vmem_limit_bytes=56 * 1024 * 1024
        ),
        name="attention",
    )(prompt_qkv, prompt_grad, comp_qkv, comp_grad, lengths, keep_mask)
    return pl.pallas_call(
        place,
        out_shape=tuple(jax.ShapeDtypeStruct(r.shape, r.dtype) for r in results),
        in_specs=[hbm] * 4,
        out_specs=(hbm,) * 4,
        scratch_shapes=[vmem(r.shape, r.dtype) for r in results] + [dma((2, 4))],
        compiler_params=pltpu.CompilerParams(vmem_limit_bytes=56 * 1024 * 1024),
        name="place",
    )(*results)


def solution(mesh):
    in_specs = (
        P(None, "seq", "head"),
        P("seq", "head"),
        P(None, "seq", "head", None),
        P("seq", "head", None),
        P("seq"),
        P("seq", None),
    )
    out_specs = (
        P("seq", "head"),
        P("seq", "head", None),
        P(None, "seq", "head"),
        P(None, "seq", "head", None),
    )
    return jax.shard_map(local, mesh=mesh, in_specs=in_specs, out_specs=out_specs, check_vma=False)
```

```python
import functools
import math

import jax
import jax.numpy as jnp
from jax import lax
from jax.experimental import pallas as pl
from jax.experimental.pallas import tpu as pltpu
from jax.sharding import PartitionSpec as P

MESH = pl.DeviceIdType.MESH
BF16 = jnp.bfloat16
F32 = jnp.float32

HEAD_DIM = 128
FACTOR = 1.0 / math.sqrt(HEAD_DIM)
EXP2_FACTOR = FACTOR * math.log2(math.e)
MASKED = -1e30

SLOTS = 256
COMP_ROWS = 2 * SLOTS
OWN = 64
BLOCK = 2 * OWN
ROWS = COMP_ROWS + BLOCK
WIDTH = 256
PROMPT = 2048
CHUNK = 512
STEP = 256
TOKENS = 32
PEERS = 16
SIDE = PEERS // 2


def dot_nt(a, b):
    return lax.dot_general(a, b, (((1,), (1,)), ((), ())), preferred_element_type=F32)


def dot_nn(a, b):
    return lax.dot_general(a, b, (((1,), (0,)), ((), ())), preferred_element_type=F32)


def dot_tn(a, b):
    return lax.dot_general(a, b, (((0,), (0,)), ((), ())), preferred_element_type=F32)


def fold_rows(value, op):
    return op(value.reshape(value.shape[0] // 8, 8, value.shape[1]), axis=0)


def await_bytes(ref, sem):
    pltpu.make_async_copy(ref, ref, sem).wait()


def remote(src, dst, send_sem, recv_sem, device):
    copy = pltpu.make_async_remote_copy(
        src_ref=src,
        dst_ref=dst,
        send_sem=send_sem,
        recv_sem=recv_sem,
        device_id=device,
        device_id_type=MESH,
    )
    copy.start()


def kernel(
    pqkv, pgrad, cqkv, cgrad, lengths, mask,
    pout, cout, pdqkv, cdqkv,
    kv, x, v01, e, eb, en, enb, dsb, tops, ot, gp, dl, dp, y_buf, ra, rb, rc, rd, za, zb, zc, zd,
    local_sem, pair_send, pair_recv, swap_send, swap_recv, ag_send, ag_recv,
    rs_send, rs_recv, back_send, back_recv, last_send, last_recv,
):
    seq = lax.axis_index("seq")
    head = lax.axis_index("head")
    y = seq // 8
    z = (seq // 2) % 4
    core = seq % 2
    other = 1 - core

    def at(yy, zz, cc):
        return ((yy * 4 + zz) * 2 + cc, head)

    partner = at(y, z, other)
    y_right, y_left, y_far = (y + 1) % 4, (y + 3) % 4, (y + 2) % 4
    z_right, z_left, z_far = (z + 1) % 4, (z + 3) % 4, (z + 2) % 4
    to_y_right, to_y_left = at(y_right, z, core), at(y_left, z, core)
    to_z_right, to_z_left = at(y, z_right, core), at(y, z_left, core)

    me = head * 2 + core

    def peer(step, cross):
        there = (head // 2 * 2 + core + step) % SIDE
        there_head = there // 2 * 2 + (head + cross) % 2
        there_core = there % 2
        device = ((y * 4 + z) * 2 + there_core, there_head)
        return device, there_head, there_core, there_head * 2 + there_core

    def rows(start, size):
        return pl.ds(pl.multiple_of(start, size), size)

    def lanes(index):
        return pl.ds(pl.multiple_of(index * WIDTH, WIDTH), WIDTH)

    own_rows = rows(seq * OWN, OWN)
    own_query = rows(COMP_ROWS + core * OWN, OWN)
    my_slots = rows(core * SLOTS + head * TOKENS, TOKENS)

    local = [
        pltpu.make_async_copy(pqkv.at[1:3, :, lanes(core)], kv.at[:, own_rows, :], local_sem.at[0]),
        pltpu.make_async_copy(pqkv.at[0, :, lanes(core)], x.at[0, own_query, :], local_sem.at[1]),
        pltpu.make_async_copy(pgrad.at[:, lanes(core)], x.at[3, own_query, :], local_sem.at[2]),
        pltpu.make_async_copy(
            cqkv.at[:, 0, :, lanes(me)], x.at[0:3, my_slots, :], local_sem.at[3]
        ),
        pltpu.make_async_copy(cgrad.at[0, :, lanes(me)], x.at[3, my_slots, :], local_sem.at[4]),
    ]
    for copy in local:
        copy.start()

    barrier = pltpu.get_barrier_semaphore()
    for device in (to_y_right, to_y_left, to_z_right, to_z_left):
        pl.semaphore_signal(barrier, inc=1, device_id=device, device_id_type=MESH)
    for cross in range(2):
        for step in range(1 - cross, SIDE):
            device = peer(step, cross)[0]
            pl.semaphore_signal(barrier, inc=1, device_id=device, device_id_type=MESH)

    position = lax.broadcasted_iota(jnp.int32, (1, SLOTS), 1)
    valid = jnp.where((position < lengths[0]) & (mask[...] == 1), 1.0, 0.0)
    v01[core] = jnp.transpose(jnp.broadcast_to(valid, (HEAD_DIM, SLOTS)))

    pl.semaphore_wait(barrier, PEERS - 1 + 4)

    for part in range(2):
        remote(
            pqkv.at[1 + part, :, lanes(other)], kv.at[part, own_rows, :],
            pair_send.at[part], pair_recv.at[part], partner,
        )

    def swap(group, cross):
        def body(step, carry):
            device, _, _, there = peer(step, cross)
            if group < 3:
                src = cqkv.at[group, 0, :, lanes(there)]
            else:
                src = cgrad.at[0, :, lanes(there)]
            dst = x.at[group, my_slots, :]
            remote(src, dst, swap_send.at[cross, group], swap_recv.at[cross, group], device)
            return carry

        lax.fori_loop(1 - cross, SIDE, body, 0)

    others = ((SIDE - 1) * TOKENS, SIDE * TOKENS)

    def await_swap(group):
        for cross in range(2):
            await_bytes(x.at[group, 0 : others[cross], :], swap_recv.at[cross, group])

    def block_at(yy, zz):
        return (yy * 4 + zz) * BLOCK

    def ag(t, start, size, slot, device):
        part = kv.at[t, rows(start, size), :]
        remote(part, part, ag_send.at[t, slot], ag_recv.at[t, slot], device)

    def ag_wait(t, start, size, slot):
        await_bytes(kv.at[t, rows(start, size), :], ag_recv.at[t, slot])

    zs = (z, z_left, z_right, z_far)

    def y_send(t, j):
        ag(t, block_at(y, zs[j]), BLOCK, 4 + 4 * j, to_y_right)
        ag(t, block_at(y, zs[j]), BLOCK, 5 + 4 * j, to_y_left)

    def y_forward(t, j):
        ag_wait(t, block_at(y_left, zs[j]), BLOCK, 4 + 4 * j)
        ag(t, block_at(y_left, zs[j]), OWN, 6 + 4 * j, to_y_right)
        ag_wait(t, block_at(y_right, zs[j]), BLOCK, 5 + 4 * j)
        ag(t, block_at(y_right, zs[j]) + OWN, OWN, 7 + 4 * j, to_y_left)

    def z_send(t):
        ag(t, block_at(y, z), BLOCK, 0, to_z_right)
        ag(t, block_at(y, z), BLOCK, 1, to_z_left)

    def z_forward(t):
        ag_wait(t, block_at(y, z_left), BLOCK, 0)
        ag(t, block_at(y, z_left), OWN, 2, to_z_right)
        ag_wait(t, block_at(y, z_right), BLOCK, 1)
        ag(t, block_at(y, z_right) + OWN, OWN, 3, to_z_left)
        if t == 0:
            z_send(1)
        y_send(t, 1)
        y_send(t, 2)

    def z_end(t):
        ag_wait(t, block_at(y, z_far), OWN, 2)
        ag_wait(t, block_at(y, z_far) + OWN, OWN, 3)
        y_send(t, 3)

    def y_end(t):
        for j in range(4):
            ag_wait(t, block_at(y_far, zs[j]), OWN, 6 + 4 * j)
            ag_wait(t, block_at(y_far, zs[j]) + OWN, OWN, 7 + 4 * j)

    def head_lanes(h):
        return slice(h * HEAD_DIM, (h + 1) * HEAD_DIM)

    def slots_of(comp):
        return slice(comp * SLOTS, (comp + 1) * SLOTS)

    def scores(yy):
        at_chunk = rows(yy * CHUNK, CHUNK)
        for h in range(2):
            score = dot_nt(kv[0, at_chunk, head_lanes(h)], x[0, :, head_lanes(h)])
            e[h, at_chunk, :] = score
            tops[h] = jnp.maximum(tops[h], fold_rows(score, jnp.max))

    swap(0, 0)
    swap(1, 0)
    remote(
        pqkv.at[0, :, lanes(other)], x.at[0, own_query, :], pair_send.at[2], pair_recv.at[2], partner
    )
    remote(
        pgrad.at[:, lanes(other)], x.at[3, own_query, :], pair_send.at[3], pair_recv.at[3], partner
    )
    remote(v01.at[core], v01.at[core], pair_send.at[4], pair_recv.at[4], partner)
    local[0].wait()
    tops[...] = jnp.full(tops.shape, MASKED, F32)
    await_bytes(kv.at[0, own_rows, :], pair_recv.at[0])
    z_send(0)
    y_send(0, 0)
    await_bytes(kv.at[1, own_rows, :], pair_recv.at[1])
    y_send(1, 0)
    z_forward(0)
    swap(0, 1)
    y_forward(0, 0)
    y_forward(1, 0)
    z_end(0)
    swap(1, 1)
    z_forward(1)
    swap(3, 0)
    swap(2, 0)
    y_forward(0, 1)
    y_forward(0, 2)
    for copy in local[1:]:
        copy.wait()
    for slot in (2, 3):
        await_bytes(x.at[0, own_query, :], pair_recv.at[slot])
    await_bytes(v01.at[other], pair_recv.at[4])
    await_swap(0)
    scores(y)
    z_end(1)
    swap(3, 1)
    swap(2, 1)
    y_forward(0, 3)
    y_forward(1, 1)
    y_forward(1, 2)
    scores(y_right)
    y_forward(1, 3)
    scores(y_left)
    y_end(0)
    scores(y_far)

    await_swap(1)
    inverses = []
    for h in range(2):
        hs = head_lanes(h)
        near_top = []
        for comp in range(2):
            near = dot_nt(x[1, slots_of(comp), hs], x[0, slots_of(comp), hs])
            okay = v01[comp] > 0.5
            near = jnp.where(jnp.concatenate([okay, okay], axis=1), near, MASKED)
            en[h, slots_of(comp), :] = near
            near_top.append(fold_rows(near, jnp.max))
        near_top.append(jnp.full((8, BLOCK), MASKED, F32))
        top = jnp.maximum(tops[h], jnp.concatenate(near_top, axis=1))
        top = jnp.max(top, axis=0, keepdims=True) * EXP2_FACTOR

        def exps(step, total):
            at_step = rows(step * STEP, STEP)
            grown = jnp.exp2(e[h, at_step, :] * EXP2_FACTOR - top)
            e[h, at_step, :] = grown
            eb[h, at_step, :] = grown.astype(BF16)
            return total + fold_rows(grown, jnp.sum)

        total = lax.fori_loop(0, PROMPT // STEP, exps, jnp.zeros((8, ROWS), F32))
        near_total = []
        for comp in range(2):
            cols = slots_of(comp)
            grown = jnp.exp2(en[h, cols, :] * EXP2_FACTOR - top[:, cols])
            en[h, cols, :] = grown
            enb[h, cols, :] = grown.astype(BF16)
            near_total.append(fold_rows(grown, jnp.sum))
        near_total.append(jnp.zeros((8, BLOCK), F32))
        total = total + jnp.concatenate(near_total, axis=1)
        inverses.append(1.0 / jnp.sum(total, axis=0, keepdims=True))

    def outs(first, second, h):
        values = [kv[1, rows(yy * CHUNK, CHUNK), head_lanes(h)] for yy in (first, second)]
        weights = [eb[h, rows(yy * CHUNK, CHUNK), :] for yy in (first, second)]
        return dot_tn(jnp.concatenate(values, axis=0), jnp.concatenate(weights, axis=0))

    for h in range(2):
        ot[h] = outs(y, y_right, h)
    y_end(1)
    for h in range(2):
        ot[h] += outs(y_left, y_far, h)
    await_swap(2)
    await_swap(3)
    for h in range(2):
        hs = head_lanes(h)
        inverse = inverses[h]
        for comp in range(2):
            cols = slots_of(comp)
            ot[h, :, cols] += dot_tn(x[2, cols, hs], enb[h, cols, :])
        out = (ot[h] * inverse).astype(BF16).astype(F32)
        y_buf[3, :, hs] = jnp.transpose(out).astype(BF16)
        cot = [x[3, slots_of(comp), hs].astype(F32) * v01[comp] for comp in range(2)]
        cot = jnp.concatenate(cot + [x[3, COMP_ROWS:ROWS, hs].astype(F32)], axis=0)
        scaled = (jnp.transpose(cot) * inverse).astype(BF16).astype(F32)
        gp[:, hs] = jnp.transpose(scaled).astype(BF16)
        dl[h] = jnp.broadcast_to(jnp.sum(scaled * out, axis=0, keepdims=True), (8, ROWS))

    def back(group):
        def body(cross, step, carry):
            device, there_head, there_core, _ = peer(step, cross)
            slots = rows(there_core * SLOTS + there_head * TOKENS, TOKENS)
            if group == 0:
                src, dst = y_buf.at[3, slots, :], cout.at[0, :, lanes(me)]
            elif group == 1:
                src, dst = y_buf.at[1:3, slots, :], cdqkv.at[1:3, 0, :, lanes(me)]
            else:
                src, dst = y_buf.at[0, slots, :], cdqkv.at[0, 0, :, lanes(me)]
            remote(src, dst, back_send.at[group], back_recv.at[group], device)
            return carry

        lax.fori_loop(0, SIDE, functools.partial(body, 1), 0)
        lax.fori_loop(1, SIDE, functools.partial(body, 0), 0)

    def gradients(zz):
        places = [rows(block_at(yy, zz), BLOCK) for yy in (y_far, y_right, y_left, y)]
        for h in range(2):
            hs = head_lanes(h)
            values = jnp.concatenate([kv[1, where, hs] for where in places], axis=0)
            weights = jnp.concatenate([e[h, where, :] for where in places], axis=0)
            rounded = jnp.concatenate([eb[h, where, :] for where in places], axis=0)
            ds = (weights * (dot_nt(values, gp[:, hs]) - dl[h, 0:1, :])).astype(BF16)
            dk = dot_nn(ds, x[0, :, hs]).astype(BF16)
            dv = dot_nn(rounded, gp[:, hs]).astype(BF16)
            for i, where in enumerate(places):
                part = slice(i * BLOCK, (i + 1) * BLOCK)
                dsb[h, where, :] = ds[part]
                dp[0, where, hs] = dk[part]
                dp[1, where, hs] = dv[part]

    def dp_rows(start, size):
        return dp.at[:, rows(start, size), :]

    def rs(part, dst, slot, device):
        remote(part, dst, rs_send.at[slot], rs_recv.at[slot], device)

    def add_half(start, arrived):
        at_half = rows(start, OWN)
        dp[:, at_half, :] = (dp[:, at_half, :].astype(F32) + arrived.astype(F32)).astype(BF16)

    z_order = (z_far, z_right, z_left, z)

    def y_first(i):
        far = block_at(y_far, z_order[i])
        rs(dp_rows(far, OWN), ra.at[i], 6 * i, to_y_right)
        rs(dp_rows(far + OWN, OWN), rb.at[i], 6 * i + 1, to_y_left)

    def y_second(i):
        right, left = block_at(y_right, z_order[i]), block_at(y_left, z_order[i])
        rs(dp_rows(right + OWN, OWN), rc.at[i, :, OWN:BLOCK, :], 6 * i + 2, to_y_right)
        rs(dp_rows(left, OWN), rd.at[i, :, 0:OWN, :], 6 * i + 3, to_y_left)

    def y_third(i):
        right, left = block_at(y_right, z_order[i]), block_at(y_left, z_order[i])
        await_bytes(ra.at[i], rs_recv.at[6 * i])
        add_half(right, ra[i])
        rs(dp_rows(right, OWN), rc.at[i, :, 0:OWN, :], 6 * i + 4, to_y_right)
        await_bytes(rb.at[i], rs_recv.at[6 * i + 1])
        add_half(left + OWN, rb[i])
        rs(dp_rows(left + OWN, OWN), rd.at[i, :, OWN:BLOCK, :], 6 * i + 5, to_y_left)

    def y_total(i):
        for slot in (2, 4):
            await_bytes(rc.at[i, :, 0:OWN, :], rs_recv.at[6 * i + slot])
        for slot in (3, 5):
            await_bytes(rd.at[i, :, 0:OWN, :], rs_recv.at[6 * i + slot])
        own = dp[:, rows(block_at(y, z_order[i]), BLOCK), :]
        return own.astype(F32) + rc[i].astype(F32) + rd[i].astype(F32)

    def z_first():
        dp[:, rows(block_at(y, z_far), BLOCK), :] = y_total(0).astype(BF16)
        rs(dp_rows(block_at(y, z_far), OWN), za, 24, to_z_right)
        rs(dp_rows(block_at(y, z_far) + OWN, OWN), zb, 25, to_z_left)

    def near_gradients():
        for h in range(2):
            hs = head_lanes(h)
            for comp in range(2):
                cols = slots_of(comp)
                grad = dot_nt(x[2, cols, hs], gp[cols, hs])
                ds = (en[h, cols, :] * (grad - dl[h, 0:1, cols])).astype(BF16)
                y_buf[1, cols, hs] = (dot_nn(ds, x[0, cols, hs]) * FACTOR).astype(BF16)
                y_buf[2, cols, hs] = dot_nn(enb[h, cols, :], gp[cols, hs]).astype(BF16)
                ot[h, :, cols] = dot_tn(x[1, cols, hs], ds)
            ot[h, :, COMP_ROWS:ROWS] = jnp.zeros((HEAD_DIM, BLOCK), F32)
        back(1)

    back(0)

    def after(step):
        y_first(step)
        y_second(step)
        if step == 0:
            near_gradients()
        else:
            y_third(step - 1)
        if step == 3:
            z_first()

    def gradient_step(step, carry):
        gradients((z + 10 - step - step // 2 + 2 * (step // 3)) % 4)
        for when in range(4):
            pl.when(step == when)(functools.partial(after, when))
        return carry

    lax.fori_loop(0, 4, gradient_step, 0)
    for h in range(2):
        ot[h] += dot_tn(kv[0, :, head_lanes(h)], dsb[h])
    for h in range(2):
        y_buf[0, :, head_lanes(h)] = jnp.transpose(ot[h] * FACTOR).astype(BF16)
    back(2)
    y_third(3)

    right_block = block_at(y, z_right)
    dp[:, rows(right_block, BLOCK), :] = y_total(1).astype(BF16)
    await_bytes(za, rs_recv.at[24])
    add_half(right_block, za[...])
    rs(dp_rows(right_block, BLOCK), zc, 26, to_z_right)
    left_block = block_at(y, z_left)
    dp[:, rows(left_block, BLOCK), :] = y_total(2).astype(BF16)
    await_bytes(zb, rs_recv.at[25])
    add_half(left_block + OWN, zb[...])
    rs(dp_rows(left_block, BLOCK), zd, 27, to_z_left)

    partner_query = rows(COMP_ROWS + other * OWN, OWN)
    my_half = lanes(core)
    remote(
        y_buf.at[3, partner_query, :], pout.at[:, my_half], last_send.at[0], last_recv.at[0], partner
    )
    remote(
        y_buf.at[0, partner_query, :], pdqkv.at[0, :, my_half], last_send.at[1], last_recv.at[1], partner
    )
    final = [
        pltpu.make_async_copy(y_buf.at[3, own_query, :], pout.at[:, my_half], local_sem.at[0]),
        pltpu.make_async_copy(y_buf.at[0, own_query, :], pdqkv.at[0, :, my_half], local_sem.at[1]),
        pltpu.make_async_copy(
            y_buf.at[0:3, my_slots, :], cdqkv.at[:, 0, :, lanes(me)], local_sem.at[2]
        ),
        pltpu.make_async_copy(y_buf.at[3, my_slots, :], cout.at[0, :, lanes(me)], local_sem.at[3]),
    ]
    for copy in final:
        copy.start()

    total = y_total(3)
    await_bytes(zc, rs_recv.at[26])
    await_bytes(zd, rs_recv.at[27])
    total = total + zc[...].astype(F32) + zd[...].astype(F32)
    mine = rows(block_at(y, z), BLOCK)
    dp[0, mine, :] = (total[0] * FACTOR).astype(BF16)
    dp[1, mine, :] = total[1].astype(BF16)
    partner_rows = rows(block_at(y, z) + other * OWN, OWN)
    remote(
        dp.at[:, partner_rows, :], pdqkv.at[1:3, :, my_half], last_send.at[2], last_recv.at[2], partner
    )
    last = pltpu.make_async_copy(dp.at[:, own_rows, :], pdqkv.at[1:3, :, my_half], local_sem.at[4])
    last.start()

    other_half = lanes(other)
    for t in range(2):
        for slot in range(20):
            size = BLOCK if slot < 2 or (slot >= 4 and slot % 4 < 2) else OWN
            await_bytes(kv.at[t, 0:size, :], ag_send.at[t, slot])
    for slot in range(28):
        await_bytes(dp.at[:, 0 : OWN if slot < 26 else BLOCK, :], rs_send.at[slot])
    for slot in range(4):
        await_bytes(x.at[0, own_query, :], pair_send.at[slot])
    await_bytes(v01.at[core], pair_send.at[4])
    for group in range(4):
        for cross in range(2):
            await_bytes(x.at[group, 0 : others[cross], :], swap_send.at[cross, group])
    sent = (PEERS - 1) * TOKENS
    for group, ref in enumerate(
        (y_buf.at[3, 0:sent, :], y_buf.at[1:3, 0:sent, :], y_buf.at[0, 0:sent, :])
    ):
        await_bytes(ref, back_send.at[group])
        await_bytes(ref, back_recv.at[group])
    await_bytes(pout.at[:, other_half], last_send.at[0])
    await_bytes(pout.at[:, other_half], last_recv.at[0])
    await_bytes(pdqkv.at[0, :, other_half], last_send.at[1])
    await_bytes(pdqkv.at[0, :, other_half], last_recv.at[1])
    await_bytes(pdqkv.at[1:3, :, other_half], last_send.at[2])
    await_bytes(pdqkv.at[1:3, :, other_half], last_recv.at[2])
    for copy in final:
        copy.wait()
    last.wait()


def place(*refs):
    sources, targets, held, sem = refs[:4], refs[4:8], refs[8:12], refs[12]
    into = [pltpu.make_async_copy(sources[i], held[i], sem.at[0, i]) for i in range(4)]
    out = [pltpu.make_async_copy(held[i], targets[i], sem.at[1, i]) for i in range(4)]
    for copy in into:
        copy.start()
    for i in range(4):
        into[i].wait()
        out[i].start()
    for copy in out:
        copy.wait()


def local(prompt_qkv, prompt_grad, comp_qkv, comp_grad, lengths, keep_mask):
    hbm = pl.BlockSpec(memory_space=pl.ANY)
    vmem = pltpu.VMEM
    dma = pltpu.SemaphoreType.DMA
    results = pl.pallas_call(
        kernel,
        out_shape=(
            jax.ShapeDtypeStruct((OWN, 2 * WIDTH), BF16),
            jax.ShapeDtypeStruct((1, TOKENS, PEERS * WIDTH), BF16),
            jax.ShapeDtypeStruct((3, OWN, 2 * WIDTH), BF16),
            jax.ShapeDtypeStruct((3, 1, TOKENS, PEERS * WIDTH), BF16),
        ),
        in_specs=[
            hbm,
            hbm,
            hbm,
            hbm,
            pl.BlockSpec(memory_space=pltpu.SMEM),
            pl.BlockSpec(memory_space=pltpu.VMEM),
        ],
        out_specs=(hbm, hbm, hbm, hbm),
        scratch_shapes=[
            vmem((2, PROMPT, WIDTH), BF16),
            vmem((4, ROWS, WIDTH), BF16),
            vmem((2, SLOTS, HEAD_DIM), F32),
            vmem((2, PROMPT, ROWS), F32),
            vmem((2, PROMPT, ROWS), BF16),
            vmem((2, COMP_ROWS, SLOTS), F32),
            vmem((2, COMP_ROWS, SLOTS), BF16),
            vmem((2, PROMPT, ROWS), BF16),
            vmem((2, 8, ROWS), F32),
            vmem((2, HEAD_DIM, ROWS), F32),
            vmem((ROWS, WIDTH), BF16),
            vmem((2, 8, ROWS), F32),
            vmem((2, PROMPT, WIDTH), BF16),
            vmem((4, ROWS, WIDTH), BF16),
            vmem((4, 2, OWN, WIDTH), BF16),
            vmem((4, 2, OWN, WIDTH), BF16),
            vmem((4, 2, BLOCK, WIDTH), BF16),
            vmem((4, 2, BLOCK, WIDTH), BF16),
            vmem((2, OWN, WIDTH), BF16),
            vmem((2, OWN, WIDTH), BF16),
            vmem((2, BLOCK, WIDTH), BF16),
            vmem((2, BLOCK, WIDTH), BF16),
            dma((5,)),
            dma((5,)),
            dma((5,)),
            dma((2, 4)),
            dma((2, 4)),
            dma((2, 20)),
            dma((2, 20)),
            dma((28,)),
            dma((28,)),
            dma((3,)),
            dma((3,)),
            dma((3,)),
            dma((3,)),
        ],
        compiler_params=pltpu.CompilerParams(
            collective_id=0, has_side_effects=True, vmem_limit_bytes=56 * 1024 * 1024
        ),
        name="attention",
    )(prompt_qkv, prompt_grad, comp_qkv, comp_grad, lengths, keep_mask)
    return pl.pallas_call(
        place,
        out_shape=tuple(jax.ShapeDtypeStruct(r.shape, r.dtype) for r in results),
        in_specs=[hbm] * 4,
        out_specs=(hbm,) * 4,
        scratch_shapes=[vmem(r.shape, r.dtype) for r in results] + [dma((2, 4))],
        compiler_params=pltpu.CompilerParams(vmem_limit_bytes=56 * 1024 * 1024),
        name="place",
    )(*results)


def solution(mesh):
    in_specs = (
        P(None, "seq", "head"),
        P("seq", "head"),
        P(None, "seq", "head", None),
        P("seq", "head", None),
        P("seq"),
        P("seq", None),
    )
    out_specs = (
        P("seq", "head"),
        P("seq", "head", None),
        P(None, "seq", "head"),
        P(None, "seq", "head", None),
    )
    return jax.shard_map(local, mesh=mesh, in_specs=in_specs, out_specs=out_specs, check_vma=False)
```

```python
import functools
import math

import jax
import jax.numpy as jnp
from jax import lax
from jax.experimental import pallas as pl
from jax.experimental.pallas import tpu as pltpu
from jax.sharding import PartitionSpec as P

MESH = pl.DeviceIdType.MESH
BF16 = jnp.bfloat16
F32 = jnp.float32

HEAD_DIM = 128
FACTOR = 1.0 / math.sqrt(HEAD_DIM)
EXP2_FACTOR = FACTOR * math.log2(math.e)
MASKED = -1e30

SLOTS = 256
COMP_ROWS = 2 * SLOTS
OWN = 64
BLOCK = 2 * OWN
ROWS = COMP_ROWS + BLOCK
PROMPT = 2048
CHUNK = 512
STEP = 512
TOKENS = 32
PEERS = 16
SIDE = PEERS // 2


def dot_nt(a, b):
    return lax.dot_general(a, b, (((1,), (1,)), ((), ())), preferred_element_type=F32)


def dot_nn(a, b):
    return lax.dot_general(a, b, (((1,), (0,)), ((), ())), preferred_element_type=F32)


def dot_tn(a, b):
    return lax.dot_general(a, b, (((0,), (0,)), ((), ())), preferred_element_type=F32)


def fold_rows(value, op):
    return op(value.reshape(value.shape[0] // 8, 8, value.shape[1]), axis=0)


def await_bytes(ref, sem):
    pltpu.make_async_copy(ref, ref, sem).wait()


def remote(src, dst, send_sem, recv_sem, device):
    copy = pltpu.make_async_remote_copy(
        src_ref=src,
        dst_ref=dst,
        send_sem=send_sem,
        recv_sem=recv_sem,
        device_id=device,
        device_id_type=MESH,
    )
    copy.start()


def kernel(
    pqkv, pgrad, cqkv, cgrad, lengths, mask,
    pout, cout, pdqkv, cdqkv,
    kv, x, v01, e, eb, en, enb, dsb, tops, ot, inv, gp, dl, dp, y_buf, ra, rb, rc, rd, za, zb, zc, zd,
    local_sem, final_sem, pair_send, pair_recv, swap_send, swap_recv, ag_send, ag_recv,
    rs_send, rs_recv, back_send, back_recv, last_send, last_recv,
):
    seq = lax.axis_index("seq")
    head = lax.axis_index("head")
    y = seq // 8
    z = (seq // 2) % 4
    core = seq % 2
    other = 1 - core

    def at(yy, zz, cc):
        return ((yy * 4 + zz) * 2 + cc, head)

    partner = at(y, z, other)
    y_right, y_left, y_far = (y + 1) % 4, (y + 3) % 4, (y + 2) % 4
    z_right, z_left, z_far = (z + 1) % 4, (z + 3) % 4, (z + 2) % 4
    to_y_right, to_y_left = at(y_right, z, core), at(y_left, z, core)
    to_z_right, to_z_left = at(y, z_right, core), at(y, z_left, core)

    me = head * 2 + core

    def peer(step, cross):
        there = (head // 2 * 2 + core + step) % SIDE
        there_head = there // 2 * 2 + (head + cross) % 2
        there_core = there % 2
        device = ((y * 4 + z) * 2 + there_core, there_head)
        return device, there_head, there_core, there_head * 2 + there_core

    def rows(start, size):
        return pl.ds(pl.multiple_of(start, size), size)

    def lanes(index, h):
        return pl.ds(pl.multiple_of((2 * index + h) * HEAD_DIM, HEAD_DIM), HEAD_DIM)

    own_rows = rows(seq * OWN, OWN)
    own_query = rows(COMP_ROWS + core * OWN, OWN)
    my_slots = rows(core * SLOTS + head * TOKENS, TOKENS)

    local = []
    for h in range(2):
        mine = (
            (pqkv.at[1:3, :, lanes(core, h)], kv.at[h, :, own_rows, :]),
            (pqkv.at[0, :, lanes(core, h)], x.at[h, 0, own_query, :]),
            (pgrad.at[:, lanes(core, h)], x.at[h, 3, own_query, :]),
            (cqkv.at[:, 0, :, lanes(me, h)], x.at[h, 0:3, my_slots, :]),
            (cgrad.at[0, :, lanes(me, h)], x.at[h, 3, my_slots, :]),
        )
        for i, (src, dst) in enumerate(mine):
            local.append(pltpu.make_async_copy(src, dst, local_sem.at[h, i]))
    for copy in local:
        copy.start()

    barrier = pltpu.get_barrier_semaphore()
    around = ((y_right, z), (y_left, z), (y, z_right), (y, z_left))
    for yy, zz in around:
        for cc in range(2):
            pl.semaphore_signal(barrier, inc=1, device_id=at(yy, zz, cc), device_id_type=MESH)
    for cross in range(2):
        for step in range(1 - cross, SIDE):
            device = peer(step, cross)[0]
            pl.semaphore_signal(barrier, inc=1, device_id=device, device_id_type=MESH)

    position = lax.broadcasted_iota(jnp.int32, (1, SLOTS), 1)
    valid = jnp.where((position < lengths[0]) & (mask[...] == 1), 1.0, 0.0)
    v01[core] = jnp.transpose(jnp.broadcast_to(valid, (HEAD_DIM, SLOTS)))

    pl.semaphore_wait(barrier, PEERS - 1 + 8)

    def swap(h, group, cross):
        def body(step, carry):
            device, _, _, there = peer(step, cross)
            if group == 0:
                src, dst = cqkv.at[0:2, 0, :, lanes(there, h)], x.at[h, 0:2, my_slots, :]
            elif group == 1:
                src, dst = cqkv.at[2, 0, :, lanes(there, h)], x.at[h, 2, my_slots, :]
            else:
                src, dst = cgrad.at[0, :, lanes(there, h)], x.at[h, 3, my_slots, :]
            sems = swap_send.at[h, cross, group], swap_recv.at[h, cross, group]
            remote(src, dst, *sems, device)
            return carry

        lax.fori_loop(1 - cross, SIDE, body, 0)

    others = ((SIDE - 1) * TOKENS, SIDE * TOKENS)

    def swapped(h, group, cross):
        arrays = (slice(0, 2), 2, 3)[group]
        return x.at[h, arrays, 0 : others[cross], :]

    def await_swap(h, group):
        for cross in range(2):
            await_bytes(swapped(h, group, cross), swap_recv.at[h, cross, group])

    def block_at(yy, zz):
        return (yy * 4 + zz) * BLOCK

    def held(s, start, size):
        return kv.at[s // 2, s % 2, rows(start, size), :]

    def ag(s, start, size, slot, device):
        part = held(s, start, size)
        remote(part, part, ag_send.at[s, slot], ag_recv.at[s, slot], device)

    def ag_wait(s, start, size, slot):
        await_bytes(held(s, start, size), ag_recv.at[s, slot])

    def own_part(s, device_core, send_slot, recv_sem, device):
        src = pqkv.at[1 + s % 2, :, lanes(device_core, s // 2)]
        remote(src, held(s, seq * OWN, OWN), ag_send.at[s, send_slot], recv_sem, device)

    def own_pair(s):
        remote(
            pqkv.at[1 + s % 2, :, lanes(other, s // 2)], held(s, seq * OWN, OWN),
            pair_send.at[s], pair_recv.at[s], partner,
        )

    def own_z(s):
        for cc in range(2):
            own_part(s, cc, cc, ag_recv.at[s, core], at(y, z_right, cc))
            own_part(s, cc, 2 + cc, ag_recv.at[s, 2 + core], at(y, z_left, cc))

    def own_y(s):
        for cc in range(2):
            own_part(s, cc, 6 + cc, ag_recv.at[s, 6 + core], at(y_right, z, cc))
            own_part(s, cc, 8 + cc, ag_recv.at[s, 8 + core], at(y_left, z, cc))

    zs = (z, z_left, z_right, z_far)

    def y_send(s, j):
        ag(s, block_at(y, zs[j]), BLOCK, 8 + 4 * j, to_y_right)
        ag(s, block_at(y, zs[j]), BLOCK, 9 + 4 * j, to_y_left)

    def z_forward(s):
        left, right = block_at(y, z_left), block_at(y, z_right)
        ag_wait(s, left, OWN, 0)
        ag(s, left, OWN, 4, to_z_right)
        ag_wait(s, right + OWN, OWN, 3)
        ag(s, right + OWN, OWN, 5, to_z_left)
        ag_wait(s, left + OWN, OWN, 1)
        y_send(s, 1)
        ag_wait(s, right, OWN, 2)
        y_send(s, 2)

    def z_end(s):
        ag_wait(s, block_at(y, z_far), OWN, 4)
        ag_wait(s, block_at(y, z_far) + OWN, OWN, 5)
        y_send(s, 3)

    def y_forward(s, j):
        left, right = block_at(y_left, zs[j]), block_at(y_right, zs[j])
        if j == 0:
            ag_wait(s, left, OWN, 6)
            ag(s, left, OWN, 10, to_y_right)
            ag_wait(s, right + OWN, OWN, 9)
            ag(s, right + OWN, OWN, 11, to_y_left)
            ag_wait(s, left + OWN, OWN, 7)
            ag_wait(s, right, OWN, 8)
        else:
            ag_wait(s, left, BLOCK, 8 + 4 * j)
            ag(s, left, OWN, 10 + 4 * j, to_y_right)
            ag_wait(s, right, BLOCK, 9 + 4 * j)
            ag(s, right + OWN, OWN, 11 + 4 * j, to_y_left)

    def y_end(s):
        for j in range(4):
            ag_wait(s, block_at(y_far, zs[j]), OWN, 10 + 4 * j)
            ag_wait(s, block_at(y_far, zs[j]) + OWN, OWN, 11 + 4 * j)

    def slots_of(comp):
        return slice(comp * SLOTS, (comp + 1) * SLOTS)

    def scores(h, yy):
        at_chunk = rows(yy * CHUNK, CHUNK)
        score = dot_nt(kv[h, 0, at_chunk, :], x[h, 0])
        e[h, at_chunk, :] = score
        tops[h] = jnp.maximum(tops[h], fold_rows(score, jnp.max))

    def exponentials(h):
        near_top = []
        for comp in range(2):
            near = dot_nt(x[h, 1, slots_of(comp), :], x[h, 0, slots_of(comp), :])
            okay = v01[comp] > 0.5
            near = jnp.where(jnp.concatenate([okay, okay], axis=1), near, MASKED)
            en[h, slots_of(comp), :] = near
            near_top.append(fold_rows(near, jnp.max))
        near_top.append(jnp.full((8, BLOCK), MASKED, F32))
        top = jnp.maximum(tops[h], jnp.concatenate(near_top, axis=1))
        top = jnp.max(top, axis=0, keepdims=True) * EXP2_FACTOR

        def exps(step, total):
            at_step = rows(step * STEP, STEP)
            grown = jnp.exp2(e[h, at_step, :] * EXP2_FACTOR - top)
            e[h, at_step, :] = grown
            eb[h, at_step, :] = grown.astype(BF16)
            return total + fold_rows(grown, jnp.sum)

        total = lax.fori_loop(0, PROMPT // STEP, exps, jnp.zeros((8, ROWS), F32))
        near_total = []
        for comp in range(2):
            cols = slots_of(comp)
            grown = jnp.exp2(en[h, cols, :] * EXP2_FACTOR - top[:, cols])
            en[h, cols, :] = grown
            enb[h, cols, :] = grown.astype(BF16)
            near_total.append(fold_rows(grown, jnp.sum))
        near_total.append(jnp.zeros((8, BLOCK), F32))
        total = total + jnp.concatenate(near_total, axis=1)
        inverse = 1.0 / jnp.sum(total, axis=0, keepdims=True)
        inv[h] = jnp.broadcast_to(inverse, (8, ROWS))

    def outputs(h):
        inverse = inv[h, 0:1, :]
        ot[h] = dot_tn(kv[h, 1], eb[h])
        await_swap(h, 1)
        await_swap(h, 2)
        for comp in range(2):
            cols = slots_of(comp)
            ot[h, :, cols] += dot_tn(x[h, 2, cols, :], enb[h, cols, :])
        out = (ot[h] * inverse).astype(BF16).astype(F32)
        y_buf[h, 3] = jnp.transpose(out).astype(BF16)
        cot = [x[h, 3, slots_of(comp), :].astype(F32) * v01[comp] for comp in range(2)]
        cot = jnp.concatenate(cot + [x[h, 3, COMP_ROWS:ROWS, :].astype(F32)], axis=0)
        scaled = (jnp.transpose(cot) * inverse).astype(BF16).astype(F32)
        gp[h] = jnp.transpose(scaled).astype(BF16)
        dl[h] = jnp.broadcast_to(jnp.sum(scaled * out, axis=0, keepdims=True), (8, ROWS))
        back(h, 0)

    def back(h, group):
        def body(cross, step, carry):
            device, there_head, there_core, _ = peer(step, cross)
            slots = rows(there_core * SLOTS + there_head * TOKENS, TOKENS)
            if group == 0:
                src, dst = y_buf.at[h, 3, slots, :], cout.at[0, :, lanes(me, h)]
            else:
                src, dst = y_buf.at[h, 0:3, slots, :], cdqkv.at[:, 0, :, lanes(me, h)]
            remote(src, dst, back_send.at[h, group], back_recv.at[h, group], device)
            return carry

        lax.fori_loop(0, SIDE, functools.partial(body, 1), 0)
        lax.fori_loop(1, SIDE, functools.partial(body, 0), 0)

    def gradients(h, zz):
        places = [rows(block_at(yy, zz), BLOCK) for yy in (y_far, y_right, y_left, y)]
        values = jnp.concatenate([kv[h, 1, where, :] for where in places], axis=0)
        weights = jnp.concatenate([e[h, where, :] for where in places], axis=0)
        rounded = jnp.concatenate([eb[h, where, :] for where in places], axis=0)
        ds = (weights * (dot_nt(values, gp[h]) - dl[h, 0:1, :])).astype(BF16)
        dk = dot_nn(ds, x[h, 0]).astype(BF16)
        dv = dot_nn(rounded, gp[h]).astype(BF16)
        for i, where in enumerate(places):
            part = slice(i * BLOCK, (i + 1) * BLOCK)
            dsb[h, where, :] = ds[part]
            dp[h, 0, where, :] = dk[part]
            dp[h, 1, where, :] = dv[part]

    def rest(h):
        for comp in range(2):
            cols = slots_of(comp)
            grad = dot_nt(x[h, 2, cols, :], gp[h, cols, :])
            ds = (en[h, cols, :] * (grad - dl[h, 0:1, cols])).astype(BF16)
            y_buf[h, 1, cols, :] = (dot_nn(ds, x[h, 0, cols, :]) * FACTOR).astype(BF16)
            y_buf[h, 2, cols, :] = dot_nn(enb[h, cols, :], gp[h, cols, :]).astype(BF16)
            ot[h, :, cols] = dot_tn(x[h, 1, cols, :], ds)
        ot[h, :, COMP_ROWS:ROWS] = jnp.zeros((HEAD_DIM, BLOCK), F32)
        total = ot[h] + dot_tn(kv[h, 0], dsb[h])
        y_buf[h, 0] = jnp.transpose(total * FACTOR).astype(BF16)
        back(h, 1)

    def dp_rows(h, start, size):
        return dp.at[h, :, rows(start, size), :]

    def rs(h, part, dst, slot, device):
        remote(part, dst, rs_send.at[h, slot], rs_recv.at[h, slot], device)

    def add_half(h, start, arrived):
        at_half = rows(start, OWN)
        dp[h, :, at_half, :] = (dp[h, :, at_half, :].astype(F32) + arrived.astype(F32)).astype(BF16)

    z_order = (z_far, z_right, z_left, z)

    def y_first(h, i):
        far = block_at(y_far, z_order[i])
        rs(h, dp_rows(h, far, OWN), ra.at[h, i], 6 * i, to_y_right)
        rs(h, dp_rows(h, far + OWN, OWN), rb.at[h, i], 6 * i + 1, to_y_left)

    def y_second(h, i):
        right, left = block_at(y_right, z_order[i]), block_at(y_left, z_order[i])
        rs(h, dp_rows(h, right + OWN, OWN), rc.at[h, i, :, OWN:BLOCK, :], 6 * i + 2, to_y_right)
        rs(h, dp_rows(h, left, OWN), rd.at[h, i, :, 0:OWN, :], 6 * i + 3, to_y_left)

    def y_third(h, i):
        right, left = block_at(y_right, z_order[i]), block_at(y_left, z_order[i])
        await_bytes(ra.at[h, i], rs_recv.at[h, 6 * i])
        add_half(h, right, ra[h, i])
        rs(h, dp_rows(h, right, OWN), rc.at[h, i, :, 0:OWN, :], 6 * i + 4, to_y_right)
        await_bytes(rb.at[h, i], rs_recv.at[h, 6 * i + 1])
        add_half(h, left + OWN, rb[h, i])
        rs(h, dp_rows(h, left + OWN, OWN), rd.at[h, i, :, OWN:BLOCK, :], 6 * i + 5, to_y_left)

    def y_total(h, i):
        for slot in (2, 4):
            await_bytes(rc.at[h, i, :, 0:OWN, :], rs_recv.at[h, 6 * i + slot])
        for slot in (3, 5):
            await_bytes(rd.at[h, i, :, 0:OWN, :], rs_recv.at[h, 6 * i + slot])
        own = dp[h, :, rows(block_at(y, z_order[i]), BLOCK), :]
        return own.astype(F32) + rc[h, i].astype(F32) + rd[h, i].astype(F32)

    def z_first(h):
        far = block_at(y, z_far)
        dp[h, :, rows(far, BLOCK), :] = y_total(h, 0).astype(BF16)
        rs(h, dp_rows(h, far, OWN), za.at[h], 24, to_z_right)
        rs(h, dp_rows(h, far + OWN, OWN), zb.at[h], 25, to_z_left)

    def z_second(h, i):
        block = block_at(y, z_order[i])
        dp[h, :, rows(block, BLOCK), :] = y_total(h, i).astype(BF16)
        if i == 1:
            await_bytes(za.at[h], rs_recv.at[h, 24])
            add_half(h, block, za[h])
            rs(h, dp_rows(h, block, BLOCK), zc.at[h], 26, to_z_right)
        else:
            await_bytes(zb.at[h], rs_recv.at[h, 25])
            add_half(h, block + OWN, zb[h])
            rs(h, dp_rows(h, block, BLOCK), zd.at[h], 27, to_z_left)

    partner_query = rows(COMP_ROWS + other * OWN, OWN)
    partner_rows = rows(block_at(y, z) + other * OWN, OWN)
    final = []

    def keep(h, slot, src, dst):
        final.append(pltpu.make_async_copy(src, dst, final_sem.at[h, slot]))
        final[-1].start()

    def give(h, slot, src, dst):
        remote(src, dst, last_send.at[h, slot], last_recv.at[h, slot], partner)

    def finish_queries(h):
        mine = lanes(core, h)
        give(h, 0, y_buf.at[h, 3, partner_query, :], pout.at[:, mine])
        give(h, 1, y_buf.at[h, 0, partner_query, :], pdqkv.at[0, :, mine])
        keep(h, 0, y_buf.at[h, 3, own_query, :], pout.at[:, mine])
        keep(h, 1, y_buf.at[h, 0, own_query, :], pdqkv.at[0, :, mine])
        keep(h, 2, y_buf.at[h, 0:3, my_slots, :], cdqkv.at[:, 0, :, lanes(me, h)])
        keep(h, 3, y_buf.at[h, 3, my_slots, :], cout.at[0, :, lanes(me, h)])

    def finish_keys(h):
        total = y_total(h, 3)
        await_bytes(zc.at[h], rs_recv.at[h, 26])
        await_bytes(zd.at[h], rs_recv.at[h, 27])
        total = total + zc[h].astype(F32) + zd[h].astype(F32)
        block = rows(block_at(y, z), BLOCK)
        dp[h, 0, block, :] = (total[0] * FACTOR).astype(BF16)
        dp[h, 1, block, :] = total[1].astype(BF16)
        give(h, 2, dp.at[h, :, partner_rows, :], pdqkv.at[1:3, :, lanes(core, h)])
        keep(h, 4, dp.at[h, :, own_rows, :], pdqkv.at[1:3, :, lanes(core, h)])

    def gradient_steps(h, events):
        def body(step, carry):
            gradients(h, (z + 10 - step - step // 2 + 2 * (step // 3)) % 4)
            for when, event in enumerate(events):
                pl.when(step == when)(event)
            return carry

        lax.fori_loop(0, 4, body, 0)

    def await_pair(s):
        await_bytes(held(s, seq * OWN, OWN), pair_recv.at[s])

    def await_rest():
        for copy in local:
            copy.wait()
        for slot in range(4, 8):
            await_bytes(x.at[0, 0, own_query, :], pair_recv.at[slot])
        await_bytes(v01.at[other], pair_recv.at[8])

    def first_scores(h):
        if h == 0:
            await_rest()
        await_pair(2 * h)
        await_swap(h, 0)
        scores(h, y)

    def side_scores(h):
        scores(h, y_right)
        scores(h, y_left)

    own_z(2)
    own_y(1)
    swap(1, 2, 0)
    own_z(0)
    for h in range(2):
        remote(
            pqkv.at[0, :, lanes(other, h)], x.at[h, 0, own_query, :],
            pair_send.at[4 + h], pair_recv.at[4 + h], partner,
        )
        remote(
            pgrad.at[:, lanes(other, h)], x.at[h, 3, own_query, :],
            pair_send.at[6 + h], pair_recv.at[6 + h], partner,
        )
    remote(v01.at[core], v01.at[core], pair_send.at[8], pair_recv.at[8], partner)
    tops[...] = jnp.full(tops.shape, MASKED, F32)
    own_y(0)
    swap(1, 1, 0)
    swap(0, 0, 0)
    own_y(2)
    own_y(3)
    own_z(1)
    y_forward(1, 0)
    swap(1, 2, 1)
    y_forward(0, 0)
    own_pair(2)
    z_forward(2)
    z_forward(0)
    z_forward(1)
    y_forward(3, 0)
    own_pair(3)
    own_z(3)
    z_end(2)
    swap(0, 0, 1)
    own_pair(0)
    z_end(0)
    swap(0, 1, 0)
    z_end(1)
    y_forward(0, 2)
    z_forward(3)
    swap(0, 2, 0)
    swap(0, 1, 1)
    swap(1, 0, 0)
    y_forward(0, 1)
    y_forward(0, 3)
    swap(0, 2, 1)
    y_forward(1, 2)
    y_forward(1, 1)
    y_forward(1, 3)
    own_pair(1)
    y_forward(2, 0)
    swap(1, 1, 1)
    y_forward(2, 2)
    y_forward(2, 1)
    y_forward(2, 3)
    first_scores(0)
    z_end(3)
    side_scores(0)
    y_forward(3, 2)
    y_forward(3, 1)
    swap(1, 0, 1)
    y_end(0)
    scores(0, y_far)
    exponentials(0)
    y_end(1)
    await_pair(1)
    outputs(0)

    def head_0_step_0():
        y_forward(3, 3)
        y_first(0, 0)
        y_end(2)

    def head_0_step_1():
        pass

    def head_0_step_2():
        y_second(0, 0)

    gradient_steps(0, (head_0_step_0, head_0_step_1, head_0_step_2))
    first_scores(1)
    y_first(0, 2)
    scores(1, y_far)
    side_scores(1)
    exponentials(1)
    y_end(3)
    y_third(0, 0)
    await_pair(3)
    outputs(1)

    def head_1_step_0():
        y_first(1, 0)
        y_first(0, 1)
        rest(0)
        y_second(1, 0)
        y_third(0, 2)

    def head_1_step_1():
        y_second(0, 1)
        z_first(0)
        y_first(1, 1)

    def head_1_step_2():
        y_third(1, 0)

    gradient_steps(1, (head_1_step_0, head_1_step_1, head_1_step_2))
    y_second(0, 2)
    y_first(1, 2)
    y_third(0, 1)
    rest(1)
    y_second(1, 2)
    y_first(0, 3)
    y_second(1, 1)
    y_first(1, 3)
    y_second(0, 3)
    z_first(1)
    y_third(1, 2)
    z_second(0, 1)
    y_third(1, 1)
    z_second(0, 2)
    y_third(0, 3)
    z_second(1, 2)
    z_second(1, 1)
    y_third(1, 3)
    y_second(1, 3)
    finish_queries(0)
    finish_queries(1)
    finish_keys(0)
    finish_keys(1)

    for s in range(4):
        for slot in range(24):
            size = BLOCK if slot >= 12 and slot % 4 < 2 else OWN
            await_bytes(held(s, 0, size), ag_send.at[s, slot])
    for slot in range(8):
        await_bytes(x.at[0, 0, own_query, :], pair_send.at[slot])
    await_bytes(v01.at[core], pair_send.at[8])
    sent = (PEERS - 1) * TOKENS
    for h in range(2):
        for slot in range(28):
            await_bytes(dp_rows(h, 0, OWN if slot < 26 else BLOCK), rs_send.at[h, slot])
        for group in range(3):
            for cross in range(2):
                await_bytes(swapped(h, group, cross), swap_send.at[h, cross, group])
        for group, ref in enumerate((y_buf.at[h, 3, 0:sent, :], y_buf.at[h, 0:3, 0:sent, :])):
            await_bytes(ref, back_send.at[h, group])
            await_bytes(ref, back_recv.at[h, group])
        theirs = lanes(other, h)
        arrivals = (pout.at[:, theirs], pdqkv.at[0, :, theirs], pdqkv.at[1:3, :, theirs])
        for slot, ref in enumerate(arrivals):
            await_bytes(ref, last_send.at[h, slot])
            await_bytes(ref, last_recv.at[h, slot])
    for copy in final:
        copy.wait()


def place(*refs):
    sources, targets, held, sem = refs[:4], refs[4:8], refs[8:12], refs[12]
    into = [pltpu.make_async_copy(sources[i], held[i], sem.at[0, i]) for i in range(4)]
    out = [pltpu.make_async_copy(held[i], targets[i], sem.at[1, i]) for i in range(4)]
    for copy in into:
        copy.start()
    for i in range(4):
        into[i].wait()
        out[i].start()
    for copy in out:
        copy.wait()


def local(prompt_qkv, prompt_grad, comp_qkv, comp_grad, lengths, keep_mask):
    hbm = pl.BlockSpec(memory_space=pl.ANY)
    vmem = pltpu.VMEM
    dma = pltpu.SemaphoreType.DMA
    results = pl.pallas_call(
        kernel,
        out_shape=(
            jax.ShapeDtypeStruct((OWN, 4 * HEAD_DIM), BF16),
            jax.ShapeDtypeStruct((1, TOKENS, 2 * PEERS * HEAD_DIM), BF16),
            jax.ShapeDtypeStruct((3, OWN, 4 * HEAD_DIM), BF16),
            jax.ShapeDtypeStruct((3, 1, TOKENS, 2 * PEERS * HEAD_DIM), BF16),
        ),
        in_specs=[
            hbm,
            hbm,
            hbm,
            hbm,
            pl.BlockSpec(memory_space=pltpu.SMEM),
            pl.BlockSpec(memory_space=pltpu.VMEM),
        ],
        out_specs=(hbm, hbm, hbm, hbm),
        scratch_shapes=[
            vmem((2, 2, PROMPT, HEAD_DIM), BF16),
            vmem((2, 4, ROWS, HEAD_DIM), BF16),
            vmem((2, SLOTS, HEAD_DIM), F32),
            vmem((2, PROMPT, ROWS), F32),
            vmem((2, PROMPT, ROWS), BF16),
            vmem((2, COMP_ROWS, SLOTS), F32),
            vmem((2, COMP_ROWS, SLOTS), BF16),
            vmem((2, PROMPT, ROWS), BF16),
            vmem((2, 8, ROWS), F32),
            vmem((2, HEAD_DIM, ROWS), F32),
            vmem((2, 8, ROWS), F32),
            vmem((2, ROWS, HEAD_DIM), BF16),
            vmem((2, 8, ROWS), F32),
            vmem((2, 2, PROMPT, HEAD_DIM), BF16),
            vmem((2, 4, ROWS, HEAD_DIM), BF16),
            vmem((2, 4, 2, OWN, HEAD_DIM), BF16),
            vmem((2, 4, 2, OWN, HEAD_DIM), BF16),
            vmem((2, 4, 2, BLOCK, HEAD_DIM), BF16),
            vmem((2, 4, 2, BLOCK, HEAD_DIM), BF16),
            vmem((2, 2, OWN, HEAD_DIM), BF16),
            vmem((2, 2, OWN, HEAD_DIM), BF16),
            vmem((2, 2, BLOCK, HEAD_DIM), BF16),
            vmem((2, 2, BLOCK, HEAD_DIM), BF16),
            dma((2, 5)),
            dma((2, 5)),
            dma((9,)),
            dma((9,)),
            dma((2, 2, 3)),
            dma((2, 2, 3)),
            dma((4, 24)),
            dma((4, 24)),
            dma((2, 28)),
            dma((2, 28)),
            dma((2, 2)),
            dma((2, 2)),
            dma((2, 3)),
            dma((2, 3)),
        ],
        compiler_params=pltpu.CompilerParams(
            collective_id=0, has_side_effects=True, vmem_limit_bytes=56 * 1024 * 1024
        ),
        name="attention",
    )(prompt_qkv, prompt_grad, comp_qkv, comp_grad, lengths, keep_mask)
    return pl.pallas_call(
        place,
        out_shape=tuple(jax.ShapeDtypeStruct(r.shape, r.dtype) for r in results),
        in_specs=[hbm] * 4,
        out_specs=(hbm,) * 4,
        scratch_shapes=[vmem(r.shape, r.dtype) for r in results] + [dma((2, 4))],
        compiler_params=pltpu.CompilerParams(vmem_limit_bytes=56 * 1024 * 1024),
        name="place",
    )(*results)


def solution(mesh):
    in_specs = (
        P(None, "seq", "head"),
        P("seq", "head"),
        P(None, "seq", "head", None),
        P("seq", "head", None),
        P("seq"),
        P("seq", None),
    )
    out_specs = (
        P("seq", "head"),
        P("seq", "head", None),
        P(None, "seq", "head"),
        P(None, "seq", "head", None),
    )
    return jax.shard_map(local, mesh=mesh, in_specs=in_specs, out_specs=out_specs, check_vma=False)
```

```python
import functools
import math

import jax
import jax.numpy as jnp
from jax import lax
from jax.experimental import pallas as pl
from jax.experimental.pallas import tpu as pltpu
from jax.sharding import PartitionSpec as P

MESH = pl.DeviceIdType.MESH
BF16 = jnp.bfloat16
F32 = jnp.float32

HEAD_DIM = 128
FACTOR = 1.0 / math.sqrt(HEAD_DIM)
EXP2_FACTOR = FACTOR * math.log2(math.e)
MASKED = -1e30

SLOTS = 256
COMP_ROWS = 2 * SLOTS
OWN = 64
BLOCK = 2 * OWN
ROWS = COMP_ROWS + BLOCK
PROMPT = 2048
CHUNK = 512
STEP = 512
TOKENS = 32
PEERS = 16
SIDE = PEERS // 2


def dot_nt(a, b):
    return lax.dot_general(a, b, (((1,), (1,)), ((), ())), preferred_element_type=F32)


def dot_nn(a, b):
    return lax.dot_general(a, b, (((1,), (0,)), ((), ())), preferred_element_type=F32)


def dot_tn(a, b):
    return lax.dot_general(a, b, (((0,), (0,)), ((), ())), preferred_element_type=F32)


def fold_rows(value, op):
    return op(value.reshape(value.shape[0] // 8, 8, value.shape[1]), axis=0)


def await_bytes(ref, sem):
    pltpu.make_async_copy(ref, ref, sem).wait()


def remote(src, dst, send_sem, recv_sem, device):
    copy = pltpu.make_async_remote_copy(
        src_ref=src,
        dst_ref=dst,
        send_sem=send_sem,
        recv_sem=recv_sem,
        device_id=device,
        device_id_type=MESH,
    )
    copy.start()


def kernel(
    pqkv, pgrad, cqkv, cgrad, lengths, mask,
    pout, cout, pdqkv, cdqkv,
    kv, x, v01, e, eb, en, enb, dsb, tops, ot, inv, gp, dl, dp, y_buf, ra, rb, rc, rd, za, zb, zc, zd,
    local_sem, final_sem, pair_send, pair_recv, swap_send, swap_recv, ag_send, ag_recv,
    rs_send, rs_recv, back_send, back_recv, last_send, last_recv,
):
    seq = lax.axis_index("seq")
    head = lax.axis_index("head")
    y = seq // 8
    z = (seq // 2) % 4
    core = seq % 2
    other = 1 - core

    def at(yy, zz, cc):
        return ((yy * 4 + zz) * 2 + cc, head)

    partner = at(y, z, other)
    y_right, y_left, y_far = (y + 1) % 4, (y + 3) % 4, (y + 2) % 4
    z_right, z_left, z_far = (z + 1) % 4, (z + 3) % 4, (z + 2) % 4
    to_y_right, to_y_left = at(y_right, z, core), at(y_left, z, core)
    to_z_right, to_z_left = at(y, z_right, core), at(y, z_left, core)

    me = head * 2 + core

    def peer(step, cross):
        there = (head // 2 * 2 + core + step) % SIDE
        there_head = there // 2 * 2 + (head + cross) % 2
        there_core = there % 2
        device = ((y * 4 + z) * 2 + there_core, there_head)
        return device, there_head, there_core, there_head * 2 + there_core

    def rows(start, size):
        return pl.ds(pl.multiple_of(start, size), size)

    def lanes(index, h):
        return pl.ds(pl.multiple_of((2 * index + h) * HEAD_DIM, HEAD_DIM), HEAD_DIM)

    own_rows = rows(seq * OWN, OWN)
    own_query = rows(COMP_ROWS + core * OWN, OWN)
    my_slots = rows(core * SLOTS + head * TOKENS, TOKENS)

    local = []
    for h in range(2):
        mine = (
            (pqkv.at[1:3, :, lanes(core, h)], kv.at[h, :, own_rows, :]),
            (pqkv.at[0, :, lanes(core, h)], x.at[h, 0, own_query, :]),
            (pgrad.at[:, lanes(core, h)], x.at[h, 3, own_query, :]),
            (cqkv.at[:, 0, :, lanes(me, h)], x.at[h, 0:3, my_slots, :]),
            (cgrad.at[0, :, lanes(me, h)], x.at[h, 3, my_slots, :]),
        )
        for i, (src, dst) in enumerate(mine):
            local.append(pltpu.make_async_copy(src, dst, local_sem.at[h, i]))
    for copy in local:
        copy.start()

    barrier = pltpu.get_barrier_semaphore()
    around = ((y_right, z), (y_left, z), (y, z_right), (y, z_left))
    for yy, zz in around:
        for cc in range(2):
            pl.semaphore_signal(barrier, inc=1, device_id=at(yy, zz, cc), device_id_type=MESH)
    for cross in range(2):
        for step in range(1 - cross, SIDE):
            device = peer(step, cross)[0]
            pl.semaphore_signal(barrier, inc=1, device_id=device, device_id_type=MESH)

    position = lax.broadcasted_iota(jnp.int32, (1, SLOTS), 1)
    valid = jnp.where((position < lengths[0]) & (mask[...] == 1), 1.0, 0.0)
    v01[core] = jnp.transpose(jnp.broadcast_to(valid, (HEAD_DIM, SLOTS)))

    pl.semaphore_wait(barrier, PEERS - 1 + 8)

    def swap(h, group, cross):
        def body(step, carry):
            device, _, _, there = peer(step, cross)
            if group == 0:
                src, dst = cqkv.at[0:2, 0, :, lanes(there, h)], x.at[h, 0:2, my_slots, :]
            elif group == 1:
                src, dst = cqkv.at[2, 0, :, lanes(there, h)], x.at[h, 2, my_slots, :]
            else:
                src, dst = cgrad.at[0, :, lanes(there, h)], x.at[h, 3, my_slots, :]
            sems = swap_send.at[h, cross, group], swap_recv.at[h, cross, group]
            remote(src, dst, *sems, device)
            return carry

        lax.fori_loop(1 - cross, SIDE, body, 0)

    others = ((SIDE - 1) * TOKENS, SIDE * TOKENS)

    def swapped(h, group, cross):
        arrays = (slice(0, 2), 2, 3)[group]
        return x.at[h, arrays, 0 : others[cross], :]

    def await_swap(h, group):
        for cross in range(2):
            await_bytes(swapped(h, group, cross), swap_recv.at[h, cross, group])

    def block_at(yy, zz):
        return (yy * 4 + zz) * BLOCK

    def held(s, start, size):
        return kv.at[s // 2, s % 2, rows(start, size), :]

    def ag(s, start, size, slot, device):
        part = held(s, start, size)
        remote(part, part, ag_send.at[s, slot], ag_recv.at[s, slot], device)

    def ag_wait(s, start, size, slot):
        await_bytes(held(s, start, size), ag_recv.at[s, slot])

    def own_part(s, device_core, send_slot, recv_sem, device):
        src = pqkv.at[1 + s % 2, :, lanes(device_core, s // 2)]
        remote(src, held(s, seq * OWN, OWN), ag_send.at[s, send_slot], recv_sem, device)

    def own_pair(s):
        remote(
            pqkv.at[1 + s % 2, :, lanes(other, s // 2)], held(s, seq * OWN, OWN),
            pair_send.at[s], pair_recv.at[s], partner,
        )

    def own_z(s):
        for cc in range(2):
            own_part(s, cc, cc, ag_recv.at[s, core], at(y, z_right, cc))
            own_part(s, cc, 2 + cc, ag_recv.at[s, 2 + core], at(y, z_left, cc))

    def own_y(s):
        for cc in range(2):
            own_part(s, cc, 6 + cc, ag_recv.at[s, 6 + core], at(y_right, z, cc))
            own_part(s, cc, 8 + cc, ag_recv.at[s, 8 + core], at(y_left, z, cc))

    zs = (z, z_left, z_right, z_far)

    def y_send(s, j):
        ag(s, block_at(y, zs[j]), BLOCK, 8 + 4 * j, to_y_right)
        ag(s, block_at(y, zs[j]), BLOCK, 9 + 4 * j, to_y_left)

    def z_forward(s):
        left, right = block_at(y, z_left), block_at(y, z_right)
        ag_wait(s, left, OWN, 0)
        ag(s, left, OWN, 4, to_z_right)
        ag_wait(s, right + OWN, OWN, 3)
        ag(s, right + OWN, OWN, 5, to_z_left)
        ag_wait(s, left + OWN, OWN, 1)
        y_send(s, 1)
        ag_wait(s, right, OWN, 2)
        y_send(s, 2)

    def z_end(s):
        ag_wait(s, block_at(y, z_far), OWN, 4)
        ag_wait(s, block_at(y, z_far) + OWN, OWN, 5)
        y_send(s, 3)

    def y_forward(s, j):
        left, right = block_at(y_left, zs[j]), block_at(y_right, zs[j])
        if j == 0:
            ag_wait(s, left, OWN, 6)
            ag(s, left, OWN, 10, to_y_right)
            ag_wait(s, right + OWN, OWN, 9)
            ag(s, right + OWN, OWN, 11, to_y_left)
            ag_wait(s, left + OWN, OWN, 7)
            ag_wait(s, right, OWN, 8)
        else:
            ag_wait(s, left, BLOCK, 8 + 4 * j)
            ag(s, left, OWN, 10 + 4 * j, to_y_right)
            ag_wait(s, right, BLOCK, 9 + 4 * j)
            ag(s, right + OWN, OWN, 11 + 4 * j, to_y_left)

    def y_end(s):
        for j in range(4):
            ag_wait(s, block_at(y_far, zs[j]), OWN, 10 + 4 * j)
            ag_wait(s, block_at(y_far, zs[j]) + OWN, OWN, 11 + 4 * j)

    def slots_of(comp):
        return slice(comp * SLOTS, (comp + 1) * SLOTS)

    def scores(h, yy):
        at_chunk = rows(yy * CHUNK, CHUNK)
        score = dot_nt(kv[h, 0, at_chunk, :], x[h, 0])
        e[h, at_chunk, :] = score
        tops[h] = jnp.maximum(tops[h], fold_rows(score, jnp.max))

    def exponentials(h):
        near_top = []
        for comp in range(2):
            near = dot_nt(x[h, 1, slots_of(comp), :], x[h, 0, slots_of(comp), :])
            okay = v01[comp] > 0.5
            near = jnp.where(jnp.concatenate([okay, okay], axis=1), near, MASKED)
            en[h, slots_of(comp), :] = near
            near_top.append(fold_rows(near, jnp.max))
        near_top.append(jnp.full((8, BLOCK), MASKED, F32))
        top = jnp.maximum(tops[h], jnp.concatenate(near_top, axis=1))
        top = jnp.max(top, axis=0, keepdims=True) * EXP2_FACTOR

        def exps(step, total):
            at_step = rows(step * STEP, STEP)
            grown = jnp.exp2(e[h, at_step, :] * EXP2_FACTOR - top)
            e[h, at_step, :] = grown
            eb[h, at_step, :] = grown.astype(BF16)
            return total + fold_rows(grown, jnp.sum)

        total = lax.fori_loop(0, PROMPT // STEP, exps, jnp.zeros((8, ROWS), F32))
        near_total = []
        for comp in range(2):
            cols = slots_of(comp)
            grown = jnp.exp2(en[h, cols, :] * EXP2_FACTOR - top[:, cols])
            en[h, cols, :] = grown
            enb[h, cols, :] = grown.astype(BF16)
            near_total.append(fold_rows(grown, jnp.sum))
        near_total.append(jnp.zeros((8, BLOCK), F32))
        total = total + jnp.concatenate(near_total, axis=1)
        inverse = 1.0 / jnp.sum(total, axis=0, keepdims=True)
        inv[h] = jnp.broadcast_to(inverse, (8, ROWS))

    def outputs(h):
        inverse = inv[h, 0:1, :]
        ot[h] = dot_tn(kv[h, 1], eb[h])
        await_swap(h, 1)
        await_swap(h, 2)
        for comp in range(2):
            cols = slots_of(comp)
            ot[h, :, cols] += dot_tn(x[h, 2, cols, :], enb[h, cols, :])
        out = (ot[h] * inverse).astype(BF16).astype(F32)
        y_buf[h, 3] = jnp.transpose(out).astype(BF16)
        cot = [x[h, 3, slots_of(comp), :].astype(F32) * v01[comp] for comp in range(2)]
        cot = jnp.concatenate(cot + [x[h, 3, COMP_ROWS:ROWS, :].astype(F32)], axis=0)
        scaled = (jnp.transpose(cot) * inverse).astype(BF16).astype(F32)
        gp[h] = jnp.transpose(scaled).astype(BF16)
        dl[h] = jnp.broadcast_to(jnp.sum(scaled * out, axis=0, keepdims=True), (8, ROWS))
        back(h, 0)

    def back(h, group):
        def body(cross, step, carry):
            device, there_head, there_core, _ = peer(step, cross)
            slots = rows(there_core * SLOTS + there_head * TOKENS, TOKENS)
            if group == 0:
                src, dst = y_buf.at[h, 3, slots, :], cout.at[0, :, lanes(me, h)]
            else:
                src, dst = y_buf.at[h, 0:3, slots, :], cdqkv.at[:, 0, :, lanes(me, h)]
            remote(src, dst, back_send.at[h, group], back_recv.at[h, group], device)
            return carry

        lax.fori_loop(0, SIDE, functools.partial(body, 1), 0)
        lax.fori_loop(1, SIDE, functools.partial(body, 0), 0)

    def gradients(h, zz):
        places = [rows(block_at(yy, zz), BLOCK) for yy in (y_far, y_right, y_left, y)]
        values = jnp.concatenate([kv[h, 1, where, :] for where in places], axis=0)
        weights = jnp.concatenate([e[h, where, :] for where in places], axis=0)
        rounded = jnp.concatenate([eb[h, where, :] for where in places], axis=0)
        ds = (weights * (dot_nt(values, gp[h]) - dl[h, 0:1, :])).astype(BF16)
        dk = dot_nn(ds, x[h, 0]).astype(BF16)
        dv = dot_nn(rounded, gp[h]).astype(BF16)
        for i, where in enumerate(places):
            part = slice(i * BLOCK, (i + 1) * BLOCK)
            dsb[h, where, :] = ds[part]
            dp[h, 0, where, :] = dk[part]
            dp[h, 1, where, :] = dv[part]

    def rest(h):
        for comp in range(2):
            cols = slots_of(comp)
            grad = dot_nt(x[h, 2, cols, :], gp[h, cols, :])
            ds = (en[h, cols, :] * (grad - dl[h, 0:1, cols])).astype(BF16)
            y_buf[h, 1, cols, :] = (dot_nn(ds, x[h, 0, cols, :]) * FACTOR).astype(BF16)
            y_buf[h, 2, cols, :] = dot_nn(enb[h, cols, :], gp[h, cols, :]).astype(BF16)
            ot[h, :, cols] = dot_tn(x[h, 1, cols, :], ds)
        ot[h, :, COMP_ROWS:ROWS] = jnp.zeros((HEAD_DIM, BLOCK), F32)
        total = ot[h] + dot_tn(kv[h, 0], dsb[h])
        y_buf[h, 0] = jnp.transpose(total * FACTOR).astype(BF16)
        back(h, 1)

    def dp_rows(h, start, size):
        return dp.at[h, :, rows(start, size), :]

    def rs(h, part, dst, slot, device):
        remote(part, dst, rs_send.at[h, slot], rs_recv.at[h, slot], device)

    def add_half(h, start, arrived):
        at_half = rows(start, OWN)
        dp[h, :, at_half, :] = (dp[h, :, at_half, :].astype(F32) + arrived.astype(F32)).astype(BF16)

    z_order = (z_far, z_right, z_left, z)

    def y_first(h, i):
        far = block_at(y_far, z_order[i])
        rs(h, dp_rows(h, far, OWN), ra.at[h, i], 6 * i, to_y_right)
        rs(h, dp_rows(h, far + OWN, OWN), rb.at[h, i], 6 * i + 1, to_y_left)

    def y_second(h, i):
        right, left = block_at(y_right, z_order[i]), block_at(y_left, z_order[i])
        rs(h, dp_rows(h, right + OWN, OWN), rc.at[h, i, :, OWN:BLOCK, :], 6 * i + 2, to_y_right)
        rs(h, dp_rows(h, left, OWN), rd.at[h, i, :, 0:OWN, :], 6 * i + 3, to_y_left)

    def y_third(h, i):
        right, left = block_at(y_right, z_order[i]), block_at(y_left, z_order[i])
        await_bytes(ra.at[h, i], rs_recv.at[h, 6 * i])
        add_half(h, right, ra[h, i])
        rs(h, dp_rows(h, right, OWN), rc.at[h, i, :, 0:OWN, :], 6 * i + 4, to_y_right)
        await_bytes(rb.at[h, i], rs_recv.at[h, 6 * i + 1])
        add_half(h, left + OWN, rb[h, i])
        rs(h, dp_rows(h, left + OWN, OWN), rd.at[h, i, :, OWN:BLOCK, :], 6 * i + 5, to_y_left)

    def y_total(h, i):
        for slot in (2, 4):
            await_bytes(rc.at[h, i, :, 0:OWN, :], rs_recv.at[h, 6 * i + slot])
        for slot in (3, 5):
            await_bytes(rd.at[h, i, :, 0:OWN, :], rs_recv.at[h, 6 * i + slot])
        own = dp[h, :, rows(block_at(y, z_order[i]), BLOCK), :]
        return own.astype(F32) + rc[h, i].astype(F32) + rd[h, i].astype(F32)

    def z_first(h):
        far = block_at(y, z_far)
        dp[h, :, rows(far, BLOCK), :] = y_total(h, 0).astype(BF16)
        rs(h, dp_rows(h, far, OWN), za.at[h], 24, to_z_right)
        rs(h, dp_rows(h, far + OWN, OWN), zb.at[h], 25, to_z_left)

    def z_second(h, i):
        block = block_at(y, z_order[i])
        dp[h, :, rows(block, BLOCK), :] = y_total(h, i).astype(BF16)
        if i == 1:
            await_bytes(za.at[h], rs_recv.at[h, 24])
            add_half(h, block, za[h])
            rs(h, dp_rows(h, block, BLOCK), zc.at[h], 26, to_z_right)
        else:
            await_bytes(zb.at[h], rs_recv.at[h, 25])
            add_half(h, block + OWN, zb[h])
            rs(h, dp_rows(h, block, BLOCK), zd.at[h], 27, to_z_left)

    partner_query = rows(COMP_ROWS + other * OWN, OWN)
    partner_rows = rows(block_at(y, z) + other * OWN, OWN)
    final = []

    def keep(h, slot, src, dst):
        final.append(pltpu.make_async_copy(src, dst, final_sem.at[h, slot]))
        final[-1].start()

    def give(h, slot, src, dst):
        remote(src, dst, last_send.at[h, slot], last_recv.at[h, slot], partner)

    def finish_queries(h):
        mine = lanes(core, h)
        give(h, 0, y_buf.at[h, 3, partner_query, :], pout.at[:, mine])
        give(h, 1, y_buf.at[h, 0, partner_query, :], pdqkv.at[0, :, mine])
        keep(h, 0, y_buf.at[h, 3, own_query, :], pout.at[:, mine])
        keep(h, 1, y_buf.at[h, 0, own_query, :], pdqkv.at[0, :, mine])
        keep(h, 2, y_buf.at[h, 0:3, my_slots, :], cdqkv.at[:, 0, :, lanes(me, h)])
        keep(h, 3, y_buf.at[h, 3, my_slots, :], cout.at[0, :, lanes(me, h)])

    def finish_keys(h):
        total = y_total(h, 3)
        await_bytes(zc.at[h], rs_recv.at[h, 26])
        await_bytes(zd.at[h], rs_recv.at[h, 27])
        total = total + zc[h].astype(F32) + zd[h].astype(F32)
        block = rows(block_at(y, z), BLOCK)
        dp[h, 0, block, :] = (total[0] * FACTOR).astype(BF16)
        dp[h, 1, block, :] = total[1].astype(BF16)
        give(h, 2, dp.at[h, :, partner_rows, :], pdqkv.at[1:3, :, lanes(core, h)])
        keep(h, 4, dp.at[h, :, own_rows, :], pdqkv.at[1:3, :, lanes(core, h)])

    def gradient_steps(h, events):
        def body(step, carry):
            gradients(h, (z + 10 - step - step // 2 + 2 * (step // 3)) % 4)
            for when, event in enumerate(events):
                pl.when(step == when)(event)
            return carry

        lax.fori_loop(0, 4, body, 0)

    def await_pair(s):
        await_bytes(held(s, seq * OWN, OWN), pair_recv.at[s])

    def await_rest():
        for copy in local:
            copy.wait()
        for slot in range(4, 8):
            await_bytes(x.at[0, 0, own_query, :], pair_recv.at[slot])
        await_bytes(v01.at[other], pair_recv.at[8])

    def first_scores(h):
        if h == 0:
            await_rest()
        await_pair(2 * h)
        await_swap(h, 0)
        scores(h, y)

    def side_scores(h):
        scores(h, y_right)
        scores(h, y_left)

    own_z(0)
    own_y(0)
    swap(0, 0, 0)
    own_y(1)
    for h in range(2):
        remote(
            pqkv.at[0, :, lanes(other, h)], x.at[h, 0, own_query, :],
            pair_send.at[4 + h], pair_recv.at[4 + h], partner,
        )
        remote(
            pgrad.at[:, lanes(other, h)], x.at[h, 3, own_query, :],
            pair_send.at[6 + h], pair_recv.at[6 + h], partner,
        )
    remote(v01.at[core], v01.at[core], pair_send.at[8], pair_recv.at[8], partner)
    tops[...] = jnp.full(tops.shape, MASKED, F32)
    swap(0, 2, 0)
    own_z(1)
    own_pair(3)
    own_pair(1)
    own_y(2)
    own_z(3)
    own_y(3)
    z_forward(0)
    y_forward(0, 0)
    own_z(2)
    y_forward(1, 0)
    z_forward(1)
    swap(0, 0, 1)
    z_forward(3)
    z_end(0)
    swap(0, 1, 0)
    y_forward(0, 2)
    z_end(1)
    own_pair(0)
    swap(1, 1, 0)
    z_forward(2)
    swap(1, 0, 0)
    own_pair(2)
    swap(0, 2, 1)
    y_forward(0, 1)
    swap(1, 2, 1)
    y_forward(0, 3)
    swap(1, 2, 0)
    y_forward(3, 2)
    y_forward(1, 2)
    y_forward(1, 1)
    swap(0, 1, 1)
    z_end(3)
    y_forward(1, 3)
    first_scores(0)
    side_scores(0)
    z_end(2)
    swap(1, 0, 1)
    y_forward(2, 2)
    y_forward(3, 1)
    y_end(0)
    scores(0, y_far)
    exponentials(0)
    y_forward(2, 1)
    swap(1, 1, 1)
    y_forward(3, 0)
    y_forward(3, 3)
    y_forward(2, 0)
    y_end(1)
    await_pair(1)
    outputs(0)
    y_forward(2, 3)

    def head_0_step_0():
        pass

    def head_0_step_1():
        y_first(0, 0)

    def head_0_step_2():
        pass

    gradient_steps(0, (head_0_step_0, head_0_step_1, head_0_step_2))
    first_scores(1)
    y_second(0, 2)
    side_scores(1)
    y_end(3)
    y_first(0, 1)
    y_second(0, 0)
    y_first(0, 2)
    y_second(0, 1)
    y_end(2)
    scores(1, y_far)
    exponentials(1)
    await_pair(3)
    outputs(1)
    y_third(0, 0)

    def head_1_step_0():
        y_first(1, 0)
        rest(0)
        y_second(1, 0)
        y_third(0, 2)

    def head_1_step_1():
        y_first(1, 1)

    def head_1_step_2():
        y_first(1, 2)
        z_first(0)
        y_third(1, 0)

    gradient_steps(1, (head_1_step_0, head_1_step_1, head_1_step_2))
    y_third(0, 1)
    y_third(1, 1)
    y_second(1, 2)
    z_first(1)
    y_second(1, 1)
    y_third(1, 2)
    z_second(0, 1)
    y_first(1, 3)
    z_second(0, 2)
    y_first(0, 3)
    z_second(1, 1)
    y_second(0, 3)
    z_second(1, 2)
    y_second(1, 3)
    y_third(1, 3)
    y_third(0, 3)
    rest(1)
    finish_queries(0)
    finish_queries(1)
    finish_keys(0)
    finish_keys(1)

    for s in range(4):
        for slot in range(24):
            size = BLOCK if slot >= 12 and slot % 4 < 2 else OWN
            await_bytes(held(s, 0, size), ag_send.at[s, slot])
    for slot in range(8):
        await_bytes(x.at[0, 0, own_query, :], pair_send.at[slot])
    await_bytes(v01.at[core], pair_send.at[8])
    sent = (PEERS - 1) * TOKENS
    for h in range(2):
        for slot in range(28):
            await_bytes(dp_rows(h, 0, OWN if slot < 26 else BLOCK), rs_send.at[h, slot])
        for group in range(3):
            for cross in range(2):
                await_bytes(swapped(h, group, cross), swap_send.at[h, cross, group])
        for group, ref in enumerate((y_buf.at[h, 3, 0:sent, :], y_buf.at[h, 0:3, 0:sent, :])):
            await_bytes(ref, back_send.at[h, group])
            await_bytes(ref, back_recv.at[h, group])
        theirs = lanes(other, h)
        arrivals = (pout.at[:, theirs], pdqkv.at[0, :, theirs], pdqkv.at[1:3, :, theirs])
        for slot, ref in enumerate(arrivals):
            await_bytes(ref, last_send.at[h, slot])
            await_bytes(ref, last_recv.at[h, slot])
    for copy in final:
        copy.wait()


def place(*refs):
    sources, targets, sem = refs[:4], refs[4:8], refs[8]
    copies = [pltpu.make_async_copy(sources[i], targets[i], sem.at[i]) for i in range(4)]
    for copy in copies:
        copy.start()
    for copy in copies:
        copy.wait()


def local(prompt_qkv, prompt_grad, comp_qkv, comp_grad, lengths, keep_mask):
    hbm = pl.BlockSpec(memory_space=pl.ANY)
    vmem = pltpu.VMEM
    dma = pltpu.SemaphoreType.DMA
    results = pl.pallas_call(
        kernel,
        out_shape=(
            vmem((OWN, 4 * HEAD_DIM), BF16),
            vmem((1, TOKENS, 2 * PEERS * HEAD_DIM), BF16),
            vmem((3, OWN, 4 * HEAD_DIM), BF16),
            vmem((3, 1, TOKENS, 2 * PEERS * HEAD_DIM), BF16),
        ),
        in_specs=[
            hbm,
            hbm,
            hbm,
            hbm,
            pl.BlockSpec(memory_space=pltpu.SMEM),
            pl.BlockSpec(memory_space=pltpu.VMEM),
        ],
        out_specs=(pl.BlockSpec(memory_space=vmem),) * 4,
        scratch_shapes=[
            vmem((2, 2, PROMPT, HEAD_DIM), BF16),
            vmem((2, 4, ROWS, HEAD_DIM), BF16),
            vmem((2, SLOTS, HEAD_DIM), F32),
            vmem((2, PROMPT, ROWS), F32),
            vmem((2, PROMPT, ROWS), BF16),
            vmem((2, COMP_ROWS, SLOTS), F32),
            vmem((2, COMP_ROWS, SLOTS), BF16),
            vmem((2, PROMPT, ROWS), BF16),
            vmem((2, 8, ROWS), F32),
            vmem((2, HEAD_DIM, ROWS), F32),
            vmem((2, 8, ROWS), F32),
            vmem((2, ROWS, HEAD_DIM), BF16),
            vmem((2, 8, ROWS), F32),
            vmem((2, 2, PROMPT, HEAD_DIM), BF16),
            vmem((2, 4, ROWS, HEAD_DIM), BF16),
            vmem((2, 4, 2, OWN, HEAD_DIM), BF16),
            vmem((2, 4, 2, OWN, HEAD_DIM), BF16),
            vmem((2, 4, 2, BLOCK, HEAD_DIM), BF16),
            vmem((2, 4, 2, BLOCK, HEAD_DIM), BF16),
            vmem((2, 2, OWN, HEAD_DIM), BF16),
            vmem((2, 2, OWN, HEAD_DIM), BF16),
            vmem((2, 2, BLOCK, HEAD_DIM), BF16),
            vmem((2, 2, BLOCK, HEAD_DIM), BF16),
            dma((2, 5)),
            dma((2, 5)),
            dma((9,)),
            dma((9,)),
            dma((2, 2, 3)),
            dma((2, 2, 3)),
            dma((4, 24)),
            dma((4, 24)),
            dma((2, 28)),
            dma((2, 28)),
            dma((2, 2)),
            dma((2, 2)),
            dma((2, 3)),
            dma((2, 3)),
        ],
        compiler_params=pltpu.CompilerParams(
            collective_id=0, has_side_effects=True, vmem_limit_bytes=56 * 1024 * 1024
        ),
        name="attention",
    )(prompt_qkv, prompt_grad, comp_qkv, comp_grad, lengths, keep_mask)
    return pl.pallas_call(
        place,
        out_shape=tuple(jax.ShapeDtypeStruct(r.shape, r.dtype) for r in results),
        in_specs=[pl.BlockSpec(memory_space=vmem)] * 4,
        out_specs=(hbm,) * 4,
        scratch_shapes=[dma((4,))],
        name="place",
    )(*[pltpu.with_memory_space_constraint(r, vmem) for r in results])


def solution(mesh):
    in_specs = (
        P(None, "seq", "head"),
        P("seq", "head"),
        P(None, "seq", "head", None),
        P("seq", "head", None),
        P("seq"),
        P("seq", None),
    )
    out_specs = (
        P("seq", "head"),
        P("seq", "head", None),
        P(None, "seq", "head"),
        P(None, "seq", "head", None),
    )
    return jax.shard_map(local, mesh=mesh, in_specs=in_specs, out_specs=out_specs, check_vma=False)
```

```python
import functools
import math

import jax
import jax.numpy as jnp
from jax import lax
from jax.experimental import pallas as pl
from jax.experimental.pallas import tpu as pltpu
from jax.sharding import PartitionSpec as P

MESH = pl.DeviceIdType.MESH
BF16 = jnp.bfloat16
F32 = jnp.float32

HEAD_DIM = 128
FACTOR = 1.0 / math.sqrt(HEAD_DIM)
EXP2_FACTOR = FACTOR * math.log2(math.e)
MASKED = -1e30

SLOTS = 256
COMP_ROWS = 2 * SLOTS
OWN = 64
BLOCK = 2 * OWN
ROWS = COMP_ROWS + BLOCK
PROMPT = 2048
CHUNK = 512
STEP = 512
TOKENS = 32
PEERS = 16
SIDE = PEERS // 2


def dot_nt(a, b):
    return lax.dot_general(a, b, (((1,), (1,)), ((), ())), preferred_element_type=F32)


def dot_nn(a, b):
    return lax.dot_general(a, b, (((1,), (0,)), ((), ())), preferred_element_type=F32)


def dot_tn(a, b):
    return lax.dot_general(a, b, (((0,), (0,)), ((), ())), preferred_element_type=F32)


def fold_rows(value, op):
    return op(value.reshape(value.shape[0] // 8, 8, value.shape[1]), axis=0)


def await_bytes(ref, sem):
    pltpu.make_async_copy(ref, ref, sem).wait()


def remote(src, dst, send_sem, recv_sem, device):
    copy = pltpu.make_async_remote_copy(
        src_ref=src,
        dst_ref=dst,
        send_sem=send_sem,
        recv_sem=recv_sem,
        device_id=device,
        device_id_type=MESH,
    )
    copy.start()


def kernel(
    pqkv, pgrad, cqkv, cgrad, lengths, mask,
    pout, cout, pdqkv, cdqkv,
    kv, x, v01, e, eb, en, enb, dsb, tops, ot, inv, gp, dl, dp, y_buf, ra, rb, rc, rd, za, zb, zc, zd,
    local_sem, final_sem, pair_send, pair_recv, swap_send, swap_recv, ag_send, ag_recv,
    rs_send, rs_recv, back_send, back_recv, last_send, last_recv,
):
    seq = lax.axis_index("seq")
    head = lax.axis_index("head")
    y = seq // 8
    z = (seq // 2) % 4
    core = seq % 2
    other = 1 - core

    def at(yy, zz, cc):
        return ((yy * 4 + zz) * 2 + cc, head)

    partner = at(y, z, other)
    y_right, y_left, y_far = (y + 1) % 4, (y + 3) % 4, (y + 2) % 4
    z_right, z_left, z_far = (z + 1) % 4, (z + 3) % 4, (z + 2) % 4
    to_y_right, to_y_left = at(y_right, z, core), at(y_left, z, core)
    to_z_right, to_z_left = at(y, z_right, core), at(y, z_left, core)

    me = head * 2 + core

    def peer(step, cross):
        there = (head // 2 * 2 + core + step) % SIDE
        there_head = there // 2 * 2 + (head + cross) % 2
        there_core = there % 2
        device = ((y * 4 + z) * 2 + there_core, there_head)
        return device, there_head, there_core, there_head * 2 + there_core

    def rows(start, size):
        return pl.ds(pl.multiple_of(start, size), size)

    def lanes(index, h):
        return pl.ds(pl.multiple_of((2 * index + h) * HEAD_DIM, HEAD_DIM), HEAD_DIM)

    own_rows = rows(seq * OWN, OWN)
    own_query = rows(COMP_ROWS + core * OWN, OWN)
    my_slots = rows(core * SLOTS + head * TOKENS, TOKENS)

    local = []
    for h in range(2):
        mine = (
            (pqkv.at[1:3, :, lanes(core, h)], kv.at[h, :, own_rows, :]),
            (pqkv.at[0, :, lanes(core, h)], x.at[h, 0, own_query, :]),
            (pgrad.at[:, lanes(core, h)], x.at[h, 3, own_query, :]),
            (cqkv.at[:, 0, :, lanes(me, h)], x.at[h, 0:3, my_slots, :]),
            (cgrad.at[0, :, lanes(me, h)], x.at[h, 3, my_slots, :]),
        )
        for i, (src, dst) in enumerate(mine):
            local.append(pltpu.make_async_copy(src, dst, local_sem.at[h, i]))
    for copy in local:
        copy.start()

    barrier = pltpu.get_barrier_semaphore()
    around = ((y_right, z), (y_left, z), (y, z_right), (y, z_left))
    for yy, zz in around:
        for cc in range(2):
            pl.semaphore_signal(barrier, inc=1, device_id=at(yy, zz, cc), device_id_type=MESH)
    for cross in range(2):
        for step in range(1 - cross, SIDE):
            device = peer(step, cross)[0]
            pl.semaphore_signal(barrier, inc=1, device_id=device, device_id_type=MESH)

    position = lax.broadcasted_iota(jnp.int32, (1, SLOTS), 1)
    valid = jnp.where((position < lengths[0]) & (mask[...] == 1), 1.0, 0.0)
    v01[core] = jnp.transpose(jnp.broadcast_to(valid, (HEAD_DIM, SLOTS)))

    pl.semaphore_wait(barrier, PEERS - 1 + 8)

    def swap(h, group, cross):
        def body(step, carry):
            device, _, _, there = peer(step, cross)
            if group == 0:
                src, dst = cqkv.at[0:2, 0, :, lanes(there, h)], x.at[h, 0:2, my_slots, :]
            elif group == 1:
                src, dst = cqkv.at[2, 0, :, lanes(there, h)], x.at[h, 2, my_slots, :]
            else:
                src, dst = cgrad.at[0, :, lanes(there, h)], x.at[h, 3, my_slots, :]
            sems = swap_send.at[h, cross, group], swap_recv.at[h, cross, group]
            remote(src, dst, *sems, device)
            return carry

        lax.fori_loop(1 - cross, SIDE, body, 0)

    others = ((SIDE - 1) * TOKENS, SIDE * TOKENS)

    def swapped(h, group, cross):
        arrays = (slice(0, 2), 2, 3)[group]
        return x.at[h, arrays, 0 : others[cross], :]

    def await_swap(h, group):
        for cross in range(2):
            await_bytes(swapped(h, group, cross), swap_recv.at[h, cross, group])

    def block_at(yy, zz):
        return (yy * 4 + zz) * BLOCK

    def held(s, start, size):
        return kv.at[s // 2, s % 2, rows(start, size), :]

    def ag(s, start, size, slot, device):
        part = held(s, start, size)
        remote(part, part, ag_send.at[s, slot], ag_recv.at[s, slot], device)

    def ag_wait(s, start, size, slot):
        await_bytes(held(s, start, size), ag_recv.at[s, slot])

    def own_part(s, device_core, send_slot, recv_sem, device):
        src = pqkv.at[1 + s % 2, :, lanes(device_core, s // 2)]
        remote(src, held(s, seq * OWN, OWN), ag_send.at[s, send_slot], recv_sem, device)

    def own_pair(s):
        remote(
            pqkv.at[1 + s % 2, :, lanes(other, s // 2)], held(s, seq * OWN, OWN),
            pair_send.at[s], pair_recv.at[s], partner,
        )

    def own_z(s):
        for cc in range(2):
            own_part(s, cc, cc, ag_recv.at[s, core], at(y, z_right, cc))
            own_part(s, cc, 2 + cc, ag_recv.at[s, 2 + core], at(y, z_left, cc))

    def own_y(s):
        for cc in range(2):
            own_part(s, cc, 6 + cc, ag_recv.at[s, 6 + core], at(y_right, z, cc))
            own_part(s, cc, 8 + cc, ag_recv.at[s, 8 + core], at(y_left, z, cc))

    zs = (z, z_left, z_right, z_far)

    def y_send(s, j):
        ag(s, block_at(y, zs[j]), BLOCK, 8 + 4 * j, to_y_right)
        ag(s, block_at(y, zs[j]), BLOCK, 9 + 4 * j, to_y_left)

    def z_forward(s):
        left, right = block_at(y, z_left), block_at(y, z_right)
        ag_wait(s, left, OWN, 0)
        ag(s, left, OWN, 4, to_z_right)
        ag_wait(s, right + OWN, OWN, 3)
        ag(s, right + OWN, OWN, 5, to_z_left)
        ag_wait(s, left + OWN, OWN, 1)
        y_send(s, 1)
        ag_wait(s, right, OWN, 2)
        y_send(s, 2)

    def z_end(s):
        ag_wait(s, block_at(y, z_far), OWN, 4)
        ag_wait(s, block_at(y, z_far) + OWN, OWN, 5)
        y_send(s, 3)

    def y_forward(s, j):
        left, right = block_at(y_left, zs[j]), block_at(y_right, zs[j])
        if j == 0:
            ag_wait(s, left, OWN, 6)
            ag(s, left, OWN, 10, to_y_right)
            ag_wait(s, right + OWN, OWN, 9)
            ag(s, right + OWN, OWN, 11, to_y_left)
            ag_wait(s, left + OWN, OWN, 7)
            ag_wait(s, right, OWN, 8)
        else:
            ag_wait(s, left, BLOCK, 8 + 4 * j)
            ag(s, left, OWN, 10 + 4 * j, to_y_right)
            ag_wait(s, right, BLOCK, 9 + 4 * j)
            ag(s, right + OWN, OWN, 11 + 4 * j, to_y_left)

    def y_end(s):
        for j in range(4):
            ag_wait(s, block_at(y_far, zs[j]), OWN, 10 + 4 * j)
            ag_wait(s, block_at(y_far, zs[j]) + OWN, OWN, 11 + 4 * j)

    def slots_of(comp):
        return slice(comp * SLOTS, (comp + 1) * SLOTS)

    def scores(h, yy):
        at_chunk = rows(yy * CHUNK, CHUNK)
        score = dot_nt(kv[h, 0, at_chunk, :], x[h, 0])
        e[h, at_chunk, :] = score
        tops[h] = jnp.maximum(tops[h], fold_rows(score, jnp.max))

    def exponentials(h):
        near_top = []
        for comp in range(2):
            near = dot_nt(x[h, 1, slots_of(comp), :], x[h, 0, slots_of(comp), :])
            okay = v01[comp] > 0.5
            near = jnp.where(jnp.concatenate([okay, okay], axis=1), near, MASKED)
            en[h, slots_of(comp), :] = near
            near_top.append(fold_rows(near, jnp.max))
        near_top.append(jnp.full((8, BLOCK), MASKED, F32))
        top = jnp.maximum(tops[h], jnp.concatenate(near_top, axis=1))
        top = jnp.max(top, axis=0, keepdims=True) * EXP2_FACTOR

        def exps(step, total):
            at_step = rows(step * STEP, STEP)
            grown = jnp.exp2(e[h, at_step, :] * EXP2_FACTOR - top)
            e[h, at_step, :] = grown
            eb[h, at_step, :] = grown.astype(BF16)
            return total + fold_rows(grown, jnp.sum)

        total = lax.fori_loop(0, PROMPT // STEP, exps, jnp.zeros((8, ROWS), F32))
        near_total = []
        for comp in range(2):
            cols = slots_of(comp)
            grown = jnp.exp2(en[h, cols, :] * EXP2_FACTOR - top[:, cols])
            en[h, cols, :] = grown
            enb[h, cols, :] = grown.astype(BF16)
            near_total.append(fold_rows(grown, jnp.sum))
        near_total.append(jnp.zeros((8, BLOCK), F32))
        total = total + jnp.concatenate(near_total, axis=1)
        inverse = 1.0 / jnp.sum(total, axis=0, keepdims=True)
        inv[h] = jnp.broadcast_to(inverse, (8, ROWS))

    def outputs(h):
        inverse = inv[h, 0:1, :]
        ot[h] = dot_tn(kv[h, 1], eb[h])
        await_swap(h, 1)
        await_swap(h, 2)
        for comp in range(2):
            cols = slots_of(comp)
            ot[h, :, cols] += dot_tn(x[h, 2, cols, :], enb[h, cols, :])
        out = (ot[h] * inverse).astype(BF16).astype(F32)
        y_buf[h, 3] = jnp.transpose(out).astype(BF16)
        cot = [x[h, 3, slots_of(comp), :].astype(F32) * v01[comp] for comp in range(2)]
        cot = jnp.concatenate(cot + [x[h, 3, COMP_ROWS:ROWS, :].astype(F32)], axis=0)
        scaled = (jnp.transpose(cot) * inverse).astype(BF16).astype(F32)
        gp[h] = jnp.transpose(scaled).astype(BF16)
        dl[h] = jnp.broadcast_to(jnp.sum(scaled * out, axis=0, keepdims=True), (8, ROWS))
        back(h, 0)

    def back(h, group):
        def body(cross, step, carry):
            device, there_head, there_core, _ = peer(step, cross)
            slots = rows(there_core * SLOTS + there_head * TOKENS, TOKENS)
            if group == 0:
                src, dst = y_buf.at[h, 3, slots, :], cout.at[0, :, lanes(me, h)]
            else:
                src, dst = y_buf.at[h, 0:3, slots, :], cdqkv.at[:, 0, :, lanes(me, h)]
            remote(src, dst, back_send.at[h, group], back_recv.at[h, group], device)
            return carry

        lax.fori_loop(0, SIDE, functools.partial(body, 1), 0)
        lax.fori_loop(1, SIDE, functools.partial(body, 0), 0)

    def gradients(h, zz):
        places = [rows(block_at(yy, zz), BLOCK) for yy in (y_far, y_right, y_left, y)]
        values = jnp.concatenate([kv[h, 1, where, :] for where in places], axis=0)
        weights = jnp.concatenate([e[h, where, :] for where in places], axis=0)
        rounded = jnp.concatenate([eb[h, where, :] for where in places], axis=0)
        ds = (weights * (dot_nt(values, gp[h]) - dl[h, 0:1, :])).astype(BF16)
        dk = dot_nn(ds, x[h, 0]).astype(BF16)
        dv = dot_nn(rounded, gp[h]).astype(BF16)
        for i, where in enumerate(places):
            part = slice(i * BLOCK, (i + 1) * BLOCK)
            dsb[h, where, :] = ds[part]
            dp[h, 0, where, :] = dk[part]
            dp[h, 1, where, :] = dv[part]

    def rest(h):
        for comp in range(2):
            cols = slots_of(comp)
            grad = dot_nt(x[h, 2, cols, :], gp[h, cols, :])
            ds = (en[h, cols, :] * (grad - dl[h, 0:1, cols])).astype(BF16)
            y_buf[h, 1, cols, :] = (dot_nn(ds, x[h, 0, cols, :]) * FACTOR).astype(BF16)
            y_buf[h, 2, cols, :] = dot_nn(enb[h, cols, :], gp[h, cols, :]).astype(BF16)
            ot[h, :, cols] = dot_tn(x[h, 1, cols, :], ds)
        ot[h, :, COMP_ROWS:ROWS] = jnp.zeros((HEAD_DIM, BLOCK), F32)
        total = ot[h] + dot_tn(kv[h, 0], dsb[h])
        y_buf[h, 0] = jnp.transpose(total * FACTOR).astype(BF16)
        back(h, 1)

    def dp_rows(h, start, size):
        return dp.at[h, :, rows(start, size), :]

    def rs(h, part, dst, slot, device):
        remote(part, dst, rs_send.at[h, slot], rs_recv.at[h, slot], device)

    def add_half(h, start, arrived):
        at_half = rows(start, OWN)
        dp[h, :, at_half, :] = (dp[h, :, at_half, :].astype(F32) + arrived.astype(F32)).astype(BF16)

    z_order = (z_far, z_right, z_left, z)

    def y_first(h, i):
        far = block_at(y_far, z_order[i])
        rs(h, dp_rows(h, far, OWN), ra.at[h, i], 6 * i, to_y_right)
        rs(h, dp_rows(h, far + OWN, OWN), rb.at[h, i], 6 * i + 1, to_y_left)

    def y_second(h, i):
        right, left = block_at(y_right, z_order[i]), block_at(y_left, z_order[i])
        rs(h, dp_rows(h, right + OWN, OWN), rc.at[h, i, :, OWN:BLOCK, :], 6 * i + 2, to_y_right)
        rs(h, dp_rows(h, left, OWN), rd.at[h, i, :, 0:OWN, :], 6 * i + 3, to_y_left)

    def y_third(h, i):
        right, left = block_at(y_right, z_order[i]), block_at(y_left, z_order[i])
        await_bytes(ra.at[h, i], rs_recv.at[h, 6 * i])
        add_half(h, right, ra[h, i])
        rs(h, dp_rows(h, right, OWN), rc.at[h, i, :, 0:OWN, :], 6 * i + 4, to_y_right)
        await_bytes(rb.at[h, i], rs_recv.at[h, 6 * i + 1])
        add_half(h, left + OWN, rb[h, i])
        rs(h, dp_rows(h, left + OWN, OWN), rd.at[h, i, :, OWN:BLOCK, :], 6 * i + 5, to_y_left)

    def y_total(h, i):
        for slot in (2, 4):
            await_bytes(rc.at[h, i, :, 0:OWN, :], rs_recv.at[h, 6 * i + slot])
        for slot in (3, 5):
            await_bytes(rd.at[h, i, :, 0:OWN, :], rs_recv.at[h, 6 * i + slot])
        own = dp[h, :, rows(block_at(y, z_order[i]), BLOCK), :]
        return own.astype(F32) + rc[h, i].astype(F32) + rd[h, i].astype(F32)

    def z_first(h):
        far = block_at(y, z_far)
        dp[h, :, rows(far, BLOCK), :] = y_total(h, 0).astype(BF16)
        rs(h, dp_rows(h, far, OWN), za.at[h], 24, to_z_right)
        rs(h, dp_rows(h, far + OWN, OWN), zb.at[h], 25, to_z_left)

    def z_second(h, i):
        block = block_at(y, z_order[i])
        dp[h, :, rows(block, BLOCK), :] = y_total(h, i).astype(BF16)
        if i == 1:
            await_bytes(za.at[h], rs_recv.at[h, 24])
            add_half(h, block, za[h])
            rs(h, dp_rows(h, block, BLOCK), zc.at[h], 26, to_z_right)
        else:
            await_bytes(zb.at[h], rs_recv.at[h, 25])
            add_half(h, block + OWN, zb[h])
            rs(h, dp_rows(h, block, BLOCK), zd.at[h], 27, to_z_left)

    partner_query = rows(COMP_ROWS + other * OWN, OWN)
    partner_rows = rows(block_at(y, z) + other * OWN, OWN)
    final = []

    def keep(h, slot, src, dst):
        final.append(pltpu.make_async_copy(src, dst, final_sem.at[h, slot]))
        final[-1].start()

    def give(h, slot, src, dst):
        remote(src, dst, last_send.at[h, slot], last_recv.at[h, slot], partner)

    def finish_queries(h):
        mine = lanes(core, h)
        give(h, 0, y_buf.at[h, 3, partner_query, :], pout.at[:, mine])
        give(h, 1, y_buf.at[h, 0, partner_query, :], pdqkv.at[0, :, mine])
        keep(h, 0, y_buf.at[h, 3, own_query, :], pout.at[:, mine])
        keep(h, 1, y_buf.at[h, 0, own_query, :], pdqkv.at[0, :, mine])
        keep(h, 2, y_buf.at[h, 0:3, my_slots, :], cdqkv.at[:, 0, :, lanes(me, h)])
        keep(h, 3, y_buf.at[h, 3, my_slots, :], cout.at[0, :, lanes(me, h)])

    def finish_keys(h):
        total = y_total(h, 3)
        await_bytes(zc.at[h], rs_recv.at[h, 26])
        await_bytes(zd.at[h], rs_recv.at[h, 27])
        total = total + zc[h].astype(F32) + zd[h].astype(F32)
        block = rows(block_at(y, z), BLOCK)
        dp[h, 0, block, :] = (total[0] * FACTOR).astype(BF16)
        dp[h, 1, block, :] = total[1].astype(BF16)
        give(h, 2, dp.at[h, :, partner_rows, :], pdqkv.at[1:3, :, lanes(core, h)])
        keep(h, 4, dp.at[h, :, own_rows, :], pdqkv.at[1:3, :, lanes(core, h)])

    def gradient_steps(h, events):
        def body(step, carry):
            gradients(h, (z + 10 - step - step // 2 + 2 * (step // 3)) % 4)
            for when, event in enumerate(events):
                pl.when(step == when)(event)
            return carry

        lax.fori_loop(0, 4, body, 0)

    def await_pair(s):
        await_bytes(held(s, seq * OWN, OWN), pair_recv.at[s])

    def await_rest():
        for copy in local:
            copy.wait()
        for slot in range(4, 8):
            await_bytes(x.at[0, 0, own_query, :], pair_recv.at[slot])
        await_bytes(v01.at[other], pair_recv.at[8])

    def first_scores(h):
        if h == 0:
            await_rest()
        await_pair(2 * h)
        await_swap(h, 0)
        scores(h, y)

    def side_scores(h):
        scores(h, y_right)
        scores(h, y_left)

    own_z(0)
    own_y(0)
    swap(0, 0, 0)
    own_y(1)
    for h in range(2):
        remote(
            pqkv.at[0, :, lanes(other, h)], x.at[h, 0, own_query, :],
            pair_send.at[4 + h], pair_recv.at[4 + h], partner,
        )
        remote(
            pgrad.at[:, lanes(other, h)], x.at[h, 3, own_query, :],
            pair_send.at[6 + h], pair_recv.at[6 + h], partner,
        )
    remote(v01.at[core], v01.at[core], pair_send.at[8], pair_recv.at[8], partner)
    tops[...] = jnp.full(tops.shape, MASKED, F32)
    own_z(1)
    own_y(3)
    own_y(2)
    swap(1, 0, 0)
    own_z(2)
    own_pair(1)
    own_pair(2)
    own_pair(0)
    y_forward(0, 0)
    own_z(3)
    z_forward(0)
    y_forward(3, 0)
    y_forward(1, 0)
    z_forward(1)
    z_forward(2)
    swap(0, 0, 1)
    z_end(0)
    z_end(1)
    swap(1, 1, 0)
    swap(1, 2, 0)
    y_forward(0, 1)
    swap(0, 2, 0)
    z_end(2)
    own_pair(3)
    z_forward(3)
    swap(0, 1, 0)
    swap(0, 2, 1)
    swap(0, 1, 1)
    y_forward(0, 2)
    y_forward(0, 3)
    swap(1, 0, 1)
    y_forward(1, 1)
    y_forward(1, 3)
    y_forward(1, 2)
    swap(1, 2, 1)
    swap(1, 1, 1)
    y_forward(2, 0)
    z_end(3)
    first_scores(0)
    side_scores(0)
    y_forward(3, 1)
    y_forward(3, 2)
    y_forward(2, 1)
    y_forward(2, 3)
    y_forward(2, 2)
    y_end(0)
    scores(0, y_far)
    exponentials(0)
    y_end(1)
    await_pair(1)
    outputs(0)

    def head_0_step_0():
        y_first(0, 0)
        y_forward(3, 3)

    def head_0_step_1():
        y_first(0, 1)

    def head_0_step_2():
        y_first(0, 2)

    gradient_steps(0, (head_0_step_0, head_0_step_1, head_0_step_2))
    y_end(2)
    first_scores(1)
    scores(1, y_far)
    y_second(0, 0)
    side_scores(1)
    exponentials(1)
    y_end(3)
    y_second(0, 2)
    y_third(0, 0)
    y_second(0, 1)
    await_pair(3)
    outputs(1)
    y_third(0, 2)

    def head_1_step_0():
        y_first(1, 0)
        rest(0)
        y_second(1, 0)

    def head_1_step_1():
        y_first(1, 1)

    def head_1_step_2():
        y_first(1, 2)
        y_third(1, 0)
        z_first(0)

    gradient_steps(1, (head_1_step_0, head_1_step_1, head_1_step_2))
    y_third(0, 1)
    y_third(1, 1)
    y_second(1, 1)
    y_first(0, 3)
    z_first(1)
    y_second(1, 2)
    y_third(1, 2)
    z_second(0, 2)
    z_second(0, 1)
    y_first(1, 3)
    y_third(0, 3)
    y_second(1, 3)
    z_second(1, 1)
    z_second(1, 2)
    y_second(0, 3)
    y_third(1, 3)
    rest(1)
    finish_queries(0)
    finish_queries(1)
    finish_keys(0)
    finish_keys(1)

    for s in range(4):
        for slot in range(24):
            size = BLOCK if slot >= 12 and slot % 4 < 2 else OWN
            await_bytes(held(s, 0, size), ag_send.at[s, slot])
    for slot in range(8):
        await_bytes(x.at[0, 0, own_query, :], pair_send.at[slot])
    await_bytes(v01.at[core], pair_send.at[8])
    sent = (PEERS - 1) * TOKENS
    for h in range(2):
        for slot in range(28):
            await_bytes(dp_rows(h, 0, OWN if slot < 26 else BLOCK), rs_send.at[h, slot])
        for group in range(3):
            for cross in range(2):
                await_bytes(swapped(h, group, cross), swap_send.at[h, cross, group])
        for group, ref in enumerate((y_buf.at[h, 3, 0:sent, :], y_buf.at[h, 0:3, 0:sent, :])):
            await_bytes(ref, back_send.at[h, group])
            await_bytes(ref, back_recv.at[h, group])
        theirs = lanes(other, h)
        arrivals = (pout.at[:, theirs], pdqkv.at[0, :, theirs], pdqkv.at[1:3, :, theirs])
        for slot, ref in enumerate(arrivals):
            await_bytes(ref, last_send.at[h, slot])
            await_bytes(ref, last_recv.at[h, slot])
    for copy in final:
        copy.wait()


def place(*refs):
    sources, targets, sem = refs[:4], refs[4:8], refs[8]
    copies = [pltpu.make_async_copy(sources[i], targets[i], sem.at[i]) for i in range(4)]
    for copy in copies:
        copy.start()
    for copy in copies:
        copy.wait()


def local(prompt_qkv, prompt_grad, comp_qkv, comp_grad, lengths, keep_mask):
    hbm = pl.BlockSpec(memory_space=pl.ANY)
    vmem = pltpu.VMEM
    dma = pltpu.SemaphoreType.DMA
    results = pl.pallas_call(
        kernel,
        out_shape=(
            vmem((OWN, 4 * HEAD_DIM), BF16),
            vmem((1, TOKENS, 2 * PEERS * HEAD_DIM), BF16),
            vmem((3, OWN, 4 * HEAD_DIM), BF16),
            vmem((3, 1, TOKENS, 2 * PEERS * HEAD_DIM), BF16),
        ),
        in_specs=[
            hbm,
            hbm,
            hbm,
            hbm,
            pl.BlockSpec(memory_space=pltpu.SMEM),
            pl.BlockSpec(memory_space=pltpu.VMEM),
        ],
        out_specs=(pl.BlockSpec(memory_space=vmem),) * 4,
        scratch_shapes=[
            vmem((2, 2, PROMPT, HEAD_DIM), BF16),
            vmem((2, 4, ROWS, HEAD_DIM), BF16),
            vmem((2, SLOTS, HEAD_DIM), F32),
            vmem((2, PROMPT, ROWS), F32),
            vmem((2, PROMPT, ROWS), BF16),
            vmem((2, COMP_ROWS, SLOTS), F32),
            vmem((2, COMP_ROWS, SLOTS), BF16),
            vmem((2, PROMPT, ROWS), BF16),
            vmem((2, 8, ROWS), F32),
            vmem((2, HEAD_DIM, ROWS), F32),
            vmem((2, 8, ROWS), F32),
            vmem((2, ROWS, HEAD_DIM), BF16),
            vmem((2, 8, ROWS), F32),
            vmem((2, 2, PROMPT, HEAD_DIM), BF16),
            vmem((2, 4, ROWS, HEAD_DIM), BF16),
            vmem((2, 4, 2, OWN, HEAD_DIM), BF16),
            vmem((2, 4, 2, OWN, HEAD_DIM), BF16),
            vmem((2, 4, 2, BLOCK, HEAD_DIM), BF16),
            vmem((2, 4, 2, BLOCK, HEAD_DIM), BF16),
            vmem((2, 2, OWN, HEAD_DIM), BF16),
            vmem((2, 2, OWN, HEAD_DIM), BF16),
            vmem((2, 2, BLOCK, HEAD_DIM), BF16),
            vmem((2, 2, BLOCK, HEAD_DIM), BF16),
            dma((2, 5)),
            dma((2, 5)),
            dma((9,)),
            dma((9,)),
            dma((2, 2, 3)),
            dma((2, 2, 3)),
            dma((4, 24)),
            dma((4, 24)),
            dma((2, 28)),
            dma((2, 28)),
            dma((2, 2)),
            dma((2, 2)),
            dma((2, 3)),
            dma((2, 3)),
        ],
        compiler_params=pltpu.CompilerParams(
            collective_id=0, has_side_effects=True, vmem_limit_bytes=56 * 1024 * 1024
        ),
        name="attention",
    )(prompt_qkv, prompt_grad, comp_qkv, comp_grad, lengths, keep_mask)
    return pl.pallas_call(
        place,
        out_shape=tuple(jax.ShapeDtypeStruct(r.shape, r.dtype) for r in results),
        in_specs=[pl.BlockSpec(memory_space=vmem)] * 4,
        out_specs=(hbm,) * 4,
        scratch_shapes=[dma((4,))],
        name="place",
    )(*[pltpu.with_memory_space_constraint(r, vmem) for r in results])


def solution(mesh):
    in_specs = (
        P(None, "seq", "head"),
        P("seq", "head"),
        P(None, "seq", "head", None),
        P("seq", "head", None),
        P("seq"),
        P("seq", None),
    )
    out_specs = (
        P("seq", "head"),
        P("seq", "head", None),
        P(None, "seq", "head"),
        P(None, "seq", "head", None),
    )
    return jax.shard_map(local, mesh=mesh, in_specs=in_specs, out_specs=out_specs, check_vma=False)
```
